256 devices in a mesh: dp: 8 (over y, x_lo), ctx: 32 (over z, x_hi, core).
Axes of the slice: x: 4 (x_hi: 2, x_lo: 2; x = x_hi * 2 + x_lo), y: 4, z: 8, core: 2. Of those that a mesh axis runs over, the one named last changes fastest.
Arguments:
- query: bfloat16 [32768, 2048], P(('dp', 'ctx')), parts along dimension 0, may hold values from -128 to 128
- keys: bfloat16 [32768, 256], P(('dp', 'ctx')), parts along dimension 0, may hold values from -8 to 8
- values: bfloat16 [32768, 256], P(('dp', 'ctx')), parts along dimension 0, may hold values from -6 to 6
- attn_out: bfloat16 [32768, 2048], P(('dp', 'ctx')), parts along dimension 0, may hold values from -2 to 2
- grad_out: bfloat16 [32768, 2048], P(('dp', 'ctx')), parts along dimension 0, may hold values from -6 to 6
- log_total: float32 [16, 32768], P(None, ('dp', 'ctx')), parts along dimension 1, as said below
- doc_lengths: int32 [128], P('dp'), parts along dimension 0, may hold values from 1 to 1024, as said below
- block_order: int32 [512], P('dp'), parts along dimension 0, may hold values from 0 to 63, as said below
Outputs:
- query_grad: bfloat16 [32768, 2048], P(('dp', 'ctx')), parts along dimension 0
- key_grad: bfloat16 [32768, 256], P(('dp', 'ctx')), parts along dimension 0
- value_grad: bfloat16 [32768, 256], P(('dp', 'ctx')), parts along dimension 0
The draws below stay inside these ranges and needn't reach their ends.
There are 8 independent parts, one for each index of `dp`. The reference program is written for one: setup_inputs(seed, part) draws one part's arguments, and reference() takes and returns one part's arrays. A program takes and returns all parts, laid end to end along the dimension named above; each array names one. Nothing has to cross between parts.
Inputs may be any that keep to these rules, and one draw needn't show every extreme that they name: `doc_lengths`: 16 document lengths of at least 1 that add up to 4096; the largest is exactly 1024. `block_order`: each of the 64 blocks of 64 positions once. log_total[h, i] is the log of the sum over j with visible(i, j) = 1 of exp(score[h, i, j]).
All inputs are finite; a program needn't handle non-finite values.
Results may differ from the reference program's by a relative error of at most 0.011.
Values may be sent and summed in bfloat16 or wider, within the bound.
A program may use at most 64 MiB of HBM per device.

```python
import jax
import jax.numpy as jnp
from jax import lax

HD = 128
GROUP_Q = 8
KV_GROUPS = 2
NDOC = 16
SEQ = 4096
HALF = 64
BLOCKS = 64
MOST_DOC = 1024


def shared_keys(key):
    raw_keys = jax.random.normal(jax.random.fold_in(key, 101), (SEQ, KV_GROUPS, HD), jnp.float32)
    return jnp.clip(raw_keys, -6.0, 6.0)


def make_keys(key):
    base_keys = shared_keys(key)
    return base_keys.reshape(SEQ, KV_GROUPS * HD).astype(jnp.bfloat16)


def make_query(key):
    own_key = jax.random.fold_in(key, 5)
    own_rows = jnp.clip(jax.random.normal(own_key, (SEQ, KV_GROUPS, GROUP_Q, HD), jnp.float32), -6.0, 6.0)
    return own_rows.reshape(SEQ, KV_GROUPS * GROUP_Q * HD).astype(jnp.bfloat16)


def make_lengths(key):
    first_key = jax.random.fold_in(key, 211)
    second_key = jax.random.fold_in(key, 223)
    longest_at = jax.random.randint(first_key, (), 0, NDOC)
    weights = jax.random.randint(second_key, (NDOC - 1,), 1, 7).astype(jnp.int32)
    spare = SEQ - MOST_DOC - (NDOC - 1)
    shares = spare * weights // jnp.sum(weights)
    leftover = spare - jnp.sum(shares)
    others = 1 + shares + (jnp.arange(NDOC - 1, dtype=jnp.int32) < leftover).astype(jnp.int32)
    index_all = jnp.arange(NDOC, dtype=jnp.int32)
    source = jnp.clip(index_all - (index_all > longest_at).astype(jnp.int32), 0, NDOC - 2)
    picked = jnp.sum(jnp.where(source[:, None] == jnp.arange(NDOC - 1)[None, :], others[None, :], 0), axis=1)
    return jnp.where(index_all == longest_at, MOST_DOC, picked).astype(jnp.int32)


def make_order(key):
    return jax.random.permutation(jax.random.fold_in(key, 227), BLOCKS).astype(jnp.int32)


def draw_keys(key, part):
    return make_keys(key)


def draw_query(key, part):
    return make_query(key)


def draw_doc_lengths(key, part):
    return make_lengths(key)


def draw_block_order(key, part):
    return make_order(key)


def draw_log_total(key, part):
    query_low = lax.optimization_barrier(make_query(key))
    keys_low = lax.optimization_barrier(make_keys(key))
    query_f32 = query_low.astype(jnp.float32).reshape(SEQ, KV_GROUPS, GROUP_Q, HD)
    key_f32 = keys_low.astype(jnp.float32).reshape(SEQ, KV_GROUPS, HD)
    lengths = make_lengths(key)
    order = make_order(key)
    doc_ends = jnp.cumsum(lengths).astype(jnp.int32)
    row_ids = jnp.arange(SEQ, dtype=jnp.int32)
    onehot = ((row_ids // HALF)[:, None] == jnp.arange(BLOCKS, dtype=jnp.int32)[None, :]).astype(jnp.int32)
    tok_pos = jnp.sum(onehot * order[None, :], axis=1) * HALF + row_ids % HALF
    doc_ids = jnp.sum((doc_ends[None, :] <= tok_pos[:, None]).astype(jnp.int32), axis=1)
    width = min(512, SEQ)
    inv_root = HD ** (-0.5)

    def one_block(step_index):
        low = step_index * width
        query_rows = lax.dynamic_slice_in_dim(query_f32, low, width, 0)
        tok_q = lax.dynamic_slice_in_dim(tok_pos, low, width, 0)
        doc_q = lax.dynamic_slice_in_dim(doc_ids, low, width, 0)
        allowed = (doc_q[:, None] == doc_ids[None, :]) & (tok_pos[None, :] <= tok_q[:, None])
        scores = jnp.einsum('igqd,jgd->gqij', query_rows, key_f32, precision=lax.Precision.HIGHEST) * inv_root
        masked = jnp.where(allowed, scores, -1e+30)
        top = jnp.max(masked, axis=-1)
        total = jnp.sum(jnp.where(allowed, jnp.exp(masked - top[..., None]), 0.0), axis=-1)
        return top + jnp.log(total)
    blocks = lax.map(one_block, jnp.arange(SEQ // width, dtype=jnp.int32))
    return jnp.transpose(blocks, (1, 2, 0, 3)).reshape(KV_GROUPS * GROUP_Q, SEQ)


def steps_of(key, extent, split, low, largest):
    gain = 1.0
    for dim, shards_of in split:
        steps = jax.random.uniform(jax.random.fold_in(jax.random.fold_in(key, 6), dim), (shards_of,), jnp.float32, low / len(split), largest / len(split))
        gain = gain * jnp.repeat(jnp.exp(steps), extent[dim] // shards_of).reshape((-1,) + (1,) * (len(extent) - 1 - dim))
    return gain


def normal_values(key, dims, scale, most, split=(), kind=jnp.bfloat16):
    level = steps_of(key, dims, split, -0.22, 0.18) if split else 1.0
    values = jax.random.normal(key, dims, jnp.float32) * scale * level
    return jnp.minimum(jnp.maximum(values, -most), most).astype(kind)


def setup_inputs(seed: int = 0, part: int = 0) -> dict:
    seeds = jax.random.split(jax.random.key(seed), 9)
    part_keys = jax.random.split(jax.random.fold_in(seeds[8], part), 9)
    return {
        "query": draw_query(jax.random.fold_in(jax.random.fold_in(seeds[8], part), 71), part),
        "keys": draw_keys(jax.random.fold_in(jax.random.fold_in(seeds[8], part), 71), part),
        "values": normal_values(part_keys[2], (SEQ, KV_GROUPS * HD), 1.0, 6.0, ((0, 32),)),
        "attn_out": normal_values(part_keys[3], (SEQ, KV_GROUPS * GROUP_Q * HD), 0.3, 2.0, ((0, 32),)),
        "grad_out": normal_values(part_keys[4], (SEQ, KV_GROUPS * GROUP_Q * HD), 1.0, 6.0, ((0, 32),)),
        "log_total": draw_log_total(jax.random.fold_in(jax.random.fold_in(seeds[8], part), 71), part),
        "doc_lengths": draw_doc_lengths(jax.random.fold_in(jax.random.fold_in(seeds[8], part), 71), part),
        "block_order": draw_block_order(jax.random.fold_in(jax.random.fold_in(seeds[8], part), 71), part),
    }


def block_tokens(block_order, row_ids):
    slot_ids = jnp.arange(BLOCKS, dtype=jnp.int32)
    onehot = ((row_ids // HALF)[:, None] == slot_ids[None, :]).astype(jnp.int32)
    return (jnp.sum(onehot * block_order[None, :], axis=1) * HALF + row_ids % HALF).astype(jnp.int32)


def reference(query, keys, values, attn_out, grad_out, log_total, doc_lengths, block_order):
    inv_root = HD ** -0.5
    doc_ends = jnp.cumsum(doc_lengths).astype(jnp.int32)
    tok_pos = block_tokens(block_order, jnp.arange(SEQ, dtype=jnp.int32))
    doc_ids = jnp.sum((doc_ends[None, :] <= tok_pos[:, None]).astype(jnp.int32), axis=1).astype(jnp.int32)
    key_f32 = keys.reshape(SEQ, KV_GROUPS, HD).astype(jnp.float32)
    value_f32 = values.reshape(SEQ, KV_GROUPS, HD).astype(jnp.float32)
    lse_heads = log_total.reshape(KV_GROUPS, GROUP_Q, SEQ)
    key_width = min(512, SEQ)

    def one_block(carried, step_index):
        key_acc, value_acc = carried
        row_low = (step_index * key_width).astype(jnp.int32)

        def rows_of(array):
            part_rows = lax.dynamic_slice_in_dim(array, row_low, key_width, 0)
            return part_rows.reshape(key_width, KV_GROUPS, GROUP_Q, HD).astype(jnp.float32)

        query_f32 = rows_of(query)
        output_f32 = rows_of(attn_out)
        dout_f32 = rows_of(grad_out)
        lse_rows = lax.dynamic_slice_in_dim(lse_heads, row_low, key_width, 2)
        tok_q = lax.dynamic_slice_in_dim(tok_pos, row_low, key_width, 0)
        doc_q = lax.dynamic_slice_in_dim(doc_ids, row_low, key_width, 0)
        allowed = (doc_q[:, None] == doc_ids[None, :]) & (tok_pos[None, :] <= tok_q[:, None])
        scores = jnp.einsum('igqd,jgd->gqij', query_f32, key_f32) * inv_root
        safe = jnp.where(allowed, scores - lse_rows[..., None], 0.0)
        probs = jnp.where(allowed, jnp.exp(safe), 0.0)
        probs_low = lax.optimization_barrier(probs.astype(jnp.bfloat16)).astype(jnp.float32)
        row_delta = jnp.einsum('igqd,igqd->gqi', dout_f32, output_f32)
        dprobs = jnp.einsum('igqd,jgd->gqij', dout_f32, value_f32)
        dscore = probs * (dprobs - row_delta[..., None])
        dscore_low = lax.optimization_barrier(dscore.astype(jnp.bfloat16)).astype(jnp.float32)
        query_part = jnp.einsum('gqij,jgd->igqd', dscore_low, key_f32) * inv_root
        key_acc = key_acc + jnp.einsum('gqij,igqd->jgd', dscore_low, query_f32) * inv_root
        value_acc = value_acc + jnp.einsum('gqij,igqd->jgd', probs_low, dout_f32)
        return (key_acc, value_acc), query_part.reshape(key_width, KV_GROUPS * GROUP_Q * HD)

    zeros_acc = jnp.zeros((SEQ, KV_GROUPS, HD), jnp.float32)
    (key_acc, value_acc), query_parts = lax.scan(one_block, (zeros_acc, zeros_acc), jnp.arange(SEQ // key_width, dtype=jnp.int32))
    query_grad = query_parts.reshape(SEQ, KV_GROUPS * GROUP_Q * HD).astype(jnp.bfloat16)
    key_grad = key_acc.reshape(SEQ, KV_GROUPS * HD).astype(jnp.bfloat16)
    value_grad = value_acc.reshape(SEQ, KV_GROUPS * HD).astype(jnp.bfloat16)
    return (query_grad, key_grad, value_grad)
```

```python
import functools

import jax
import jax.numpy as jnp
from jax import lax
from jax.experimental import pallas as pl
from jax.experimental.pallas import tpu as pltpu
from jax.sharding import PartitionSpec as P

HD = 128
HEADS = 16
GROUPS = 2
HALF = 64
ROWS = 128
QUAD = 4
RING = 8
SEQ = ROWS * QUAD * RING
SHARD = ROWS * QUAD
COLS = HEADS * HD // QUAD
MEMBER_HEADS = HEADS // QUAD
TILE = 4
MESH = pl.DeviceIdType.MESH
INV_ROOT = HD ** (-0.5)
LOG2E = 1.4426950408889634
F32 = jnp.float32
BF16 = jnp.bfloat16


def place():
    me = lax.axis_index("ctx")
    return lax.axis_index("dp"), me // QUAD, lax.rem(me, QUAD)


def device(dp, z, member):
    return (dp, lax.rem(z + RING, RING) * QUAD + member)


def greet(dp, z, r):
    barrier = pltpu.get_barrier_semaphore()
    for dz in (1, -1):
        for t in range(QUAD):
            pl.semaphore_signal(barrier, inc=1, device_id=device(dp, z + dz, t), device_id_type=MESH)
    for other in range(1, QUAD):
        pl.semaphore_signal(barrier, inc=1, device_id=device(dp, z, r ^ other), device_id_type=MESH)
    return lambda: pl.semaphore_wait(barrier, 2 * QUAD + QUAD - 1)


def rows_at(start, count):
    return pl.ds(pl.multiple_of(start, count), count)


def remote(src, dst, send_sem, recv_sem, target):
    return pltpu.make_async_remote_copy(
        src_ref=src, dst_ref=dst, send_sem=send_sem, recv_sem=recv_sem, device_id=target, device_id_type=MESH
    )


def split_lanes(table, half):
    pieces = []
    for t in range(QUAD):
        heads = [
            table[t * MEMBER_HEADS + e : t * MEMBER_HEADS + e + 1, half * HALF : (half + 1) * HALF]
            for e in range(MEMBER_HEADS)
        ]
        pieces.append(jnp.concatenate(heads, axis=1))
    return jnp.concatenate(pieces, axis=0)


def gather_kernel(
    q_ref, k_ref, v_ref, o_ref, do_ref, lse_ref,
    qg_ref, dog_ref, kv_ref, ld_ref,
    o_vm, do_vm, ld_vm,
    load_sem, first_send, first_own, own_recv, other_recv, ring_send, core_send, head_send, head_recv, head_own,
):
    dp, z, r = place()
    core = lax.rem(r, 2)
    greeted = greet(dp, z, r)
    loads = [
        pltpu.make_async_copy(o_ref, o_vm, load_sem.at[0]),
        pltpu.make_async_copy(do_ref, do_vm, load_sem.at[1]),
    ]
    for c in loads:
        c.start()
    greeted()

    def kv_rows(shard, member):
        return rows_at((lax.rem(shard + RING, RING) * QUAD + member) * ROWS, ROWS)

    first = []
    mine = kv_rows(z, r)
    for i, dz in enumerate((1, -1, 0)):
        for t in range(QUAD):
            source = (v_ref if t % 2 else k_ref).at[:, (t // 2) * HD : (t // 2 + 1) * HD]
            target = kv_ref.at[t % 2, mine, :]
            copy = remote(source, target, first_send.at[i, t], own_recv.at[dz % RING, r], device(dp, z + dz, t))
            if dz:
                copy.start()
                first.append(copy)
            else:
                @pl.when(t != r)
                def _():
                    copy.start()

                @pl.when(t == r)
                def _():
                    pltpu.make_async_copy(source, target, first_own).start()

    heads = []
    for i, (src, dst) in enumerate(((q_ref, qg_ref), (do_ref, dog_ref))):
        to_rows = rows_at(r * ROWS, ROWS)
        for other in range(1, QUAD):
            t = r ^ other
            cols = rows_at(t * COLS, COLS)
            copy = remote(
                src.at[:, cols], dst.at[to_rows, :], head_send.at[i, other], head_recv.at[i, other], device(dp, z, t)
            )
            copy.start()
            heads.append(copy)
        own = pltpu.make_async_copy(src.at[:, rows_at(r * COLS, COLS)], dst.at[to_rows, :], head_own.at[i])
        own.start()
        heads.append(own)

    for c in loads:
        c.wait()
    prod = do_vm[...].astype(F32) * o_vm[...].astype(F32)
    high = prod.astype(BF16)
    low = (prod - high.astype(F32)).astype(BF16)
    head_of = lax.broadcasted_iota(jnp.int32, (HEADS, HEADS * HD), 1) // HD
    ones = (head_of == lax.broadcasted_iota(jnp.int32, (HEADS, HEADS * HD), 0)).astype(BF16)
    along = (((1,), (1,)), ((), ()))
    delta = lax.dot_general(ones, high, along, preferred_element_type=F32) + lax.dot_general(
        ones, low, along, preferred_element_type=F32
    )
    for half in range(2):
        ld_vm[0, half] = split_lanes(lse_ref[...] * LOG2E, half)
        ld_vm[1, half] = split_lanes(delta, half)
    for other in range(1, QUAD):
        copy = remote(ld_vm, ld_ref.at[r], head_send.at[2, other], head_recv.at[2, other], device(dp, z, r ^ other))
        copy.start()
        heads.append(copy)
    own = pltpu.make_async_copy(ld_vm, ld_ref.at[r], head_own.at[2])
    own.start()
    heads.append(own)

    forwards = []
    crossings = []

    def slot(k, p):
        return kv_ref.at[core, kv_rows(z - k, p), :]

    def arrived(k, p):
        piece = slot(k, p)
        remote(piece, piece, first_send.at[0, 0], own_recv.at[k, p], device(dp, z, r ^ 1)).wait_recv()
        return piece

    def forward(k, p, step, piece):
        i = 0 if step > 0 else 1
        copy = remote(piece, piece, ring_send.at[i, k, p], own_recv.at[k + step, p], device(dp, z + step, r))
        copy.start()
        forwards.append(copy)

    def cross(k, p, piece):
        copy = remote(piece, piece, core_send.at[k, p], other_recv.at[k, p], device(dp, z, r ^ 1))
        copy.start()
        crossings.append((copy, k, p))

    for k in range(1, 4):
        for p in range(QUAD):
            piece = arrived(k, p)
            if k < 3 or p < 2:
                forward(k, p, 1, piece)
            cross(k, p, piece)
            piece = arrived(RING - k, p)
            if k < 3 or p >= 2:
                forward(RING - k, p, -1, piece)
            cross(RING - k, p, piece)
        if k == 1:
            for p in range(QUAD):
                piece = slot(0, p)

                @pl.when(p != r)
                def _():
                    arrived(0, p)

                @pl.when(p == r)
                def _():
                    pltpu.make_async_copy(piece, piece, first_own).wait()

                cross(0, p, piece)
    for p in range(QUAD):
        cross(4, p, arrived(4, p))
    for copy, k, p in crossings:
        copy.wait_send()
        theirs = kv_ref.at[1 - core, kv_rows(z - k, p), :]
        remote(theirs, theirs, core_send.at[k, p], other_recv.at[k, p], device(dp, z, r ^ 1)).wait_recv()
    for copy in forwards + first:
        copy.wait_send()
    for t in range(QUAD):
        @pl.when(t != r)
        def _():
            piece = slot(0, 0)
            remote(piece, piece, first_send.at[2, t], own_recv.at[0, 0], device(dp, z, r ^ 1)).wait_send()
    for copy in heads:
        copy.wait()


def dot_tt(a, b):
    return lax.dot_general(a, b, (((1,), (1,)), ((), ())), preferred_element_type=F32)


def attend_kernel(doc_ref, order_ref, q_ref, do_ref, kv_ref, ld_ref, dq_ref, dkv_ref, acc_ref, dqt_ref, inv_ref):
    _, z, r = place()
    lanes = MEMBER_HEADS * HALF

    @pl.loop(0, SEQ // HALF)
    def _(s):
        inv_ref[order_ref[s]] = s

    acc_ref[...] = jnp.zeros_like(acc_ref)

    def query_block(member, half):
        b = order_ref[(z * QUAD + member) * 2 + half]
        low = b * HALF
        tok_q = low + lax.broadcasted_iota(jnp.int32, (1, lanes), 1) % HALF
        begin_q = jnp.zeros((1, lanes), jnp.int32)
        begin = jnp.int32(0)
        end = jnp.int32(0)
        for d in range(doc_ref.shape[0]):
            end = end + doc_ref[d]
            begin = jnp.where(end <= low, end, begin)
            begin_q = jnp.where(end <= tok_q, end, begin_q)
        tiles = (b - begin // HALF) // TILE + 1
        rows = rows_at((member * 2 + half) * HALF, HALF)
        q = jnp.concatenate([q_ref[rows, e * HD : (e + 1) * HD] for e in range(MEMBER_HEADS)], axis=0)
        do = jnp.concatenate([do_ref[rows, e * HD : (e + 1) * HD] for e in range(MEMBER_HEADS)], axis=0)
        lse = ld_ref[member, 0, half, pl.ds(r, 1), :]
        delta = ld_ref[member, 1, half, pl.ds(r, 1), :]
        dqt_ref[...] = jnp.zeros_like(dqt_ref)

        @pl.loop(0, tiles)
        def _(t):
            base = b - TILE * t - (TILE - 1)
            spans = [rows_at(inv_ref[jnp.maximum(base + j, 0)] * HALF, HALF) for j in range(TILE)]
            k = jnp.concatenate([kv_ref[0, span, :] for span in spans], axis=0)
            v = jnp.concatenate([kv_ref[1, span, :] for span in spans], axis=0)
            tok_k = base * HALF + lax.broadcasted_iota(jnp.int32, (TILE * HALF, 1), 0)
            visible = (tok_k <= tok_q) & (tok_k >= begin_q)
            score = dot_tt(k, q)
            probs = jnp.exp2(jnp.where(visible, score * (INV_ROOT * LOG2E) - lse, -1e30))
            dprobs = dot_tt(v, do)
            dscore = (probs * (dprobs - delta)).astype(BF16)
            probs_low = probs.astype(BF16)
            dv = jnp.dot(probs_low, do, preferred_element_type=F32)
            dk = jnp.dot(dscore, q, preferred_element_type=F32)
            dqt_ref[...] += lax.dot_general(k, dscore, (((0,), (0,)), ((), ())), preferred_element_type=F32)
            for j, span in enumerate(spans):
                acc_ref[0, span, :] += dk[j * HALF : (j + 1) * HALF]
                acc_ref[1, span, :] += dv[j * HALF : (j + 1) * HALF]

        dq = (dqt_ref[...].T * INV_ROOT).astype(BF16)
        for e in range(MEMBER_HEADS):
            dq_ref[rows, e * HD : (e + 1) * HD] = dq[e * HALF : (e + 1) * HALF]

    @pl.loop(0, QUAD)
    def _(member):
        for half in range(2):
            query_block(member, half)

    @pl.loop(0, SEQ // SHARD)
    def _(i):
        span = rows_at(i * SHARD, SHARD)
        dkv_ref[0, span, :] = (acc_ref[0, span, :] * INV_ROOT).astype(BF16)
        dkv_ref[1, span, :] = acc_ref[1, span, :].astype(BF16)


def reduce_kernel(
    dq_ref, dkv_ref,
    qgrad_ref, kgrad_ref, vgrad_ref,
    own_vm, other_vm, recv_vm, send_vm, last_vm, final_vm,
    load_sem, core_send, core_recv, ring_send, ring_recv, last_send, last_recv, head_send, head_recv, head_own,
):
    dp, z, r = place()
    core = lax.rem(r, 2)
    greeted = greet(dp, z, r)

    def shard(d):
        return rows_at(lax.rem(z + d + RING, RING) * SHARD, SHARD)

    def piece(d, p):
        return rows_at((lax.rem(z + d + RING, RING) * QUAD + p) * ROWS, ROWS)

    order = (4, 3, 5, 2, 6, 1, 7, 0)
    loads = {}
    for d in order:
        loads[d] = pltpu.make_async_copy(dkv_ref.at[core, shard(d), :], own_vm.at[shard(d), :], load_sem.at[d])
        loads[d].start()
    greeted()
    crossings = {}
    for d in order:
        crossings[d] = remote(
            dkv_ref.at[1 - core, shard(d), :], other_vm.at[shard(d), :], core_send.at[d], core_recv.at[d],
            device(dp, z, r ^ 1),
        )
        crossings[d].start()
    heads = []
    to_cols = rows_at(r * COLS, COLS)
    for other in range(1, QUAD):
        t = r ^ other
        copy = remote(
            dq_ref.at[rows_at(t * ROWS, ROWS), :], qgrad_ref.at[:, to_cols],
            head_send.at[other], head_recv.at[other], device(dp, z, t),
        )
        copy.start()
        heads.append(copy)
    own = pltpu.make_async_copy(dq_ref.at[rows_at(r * ROWS, ROWS), :], qgrad_ref.at[:, to_cols], head_own)
    own.start()
    heads.append(own)

    def total(d, p):
        return own_vm[piece(d, p), :].astype(F32) + other_vm[piece(d, p), :].astype(F32)

    def ready(d):
        loads[d].wait()
        crossings[d].wait_recv()

    sends = []

    def pass_on(i, s, p, value):
        here = send_vm.at[i, s, p]
        here[...] = value.astype(BF16)
        copy = remote(
            here, recv_vm.at[i, s, p], ring_send.at[i, s, p], ring_recv.at[i, s, p],
            device(dp, z + (1 - 2 * i), r),
        )
        copy.start()
        sends.append(copy)

    def came(i, s, p):
        here = recv_vm.at[i, s, p]
        remote(here, here, ring_send.at[i, s, p], ring_recv.at[i, s, p], device(dp, z, r ^ 1)).wait_recv()
        return here[...].astype(F32)

    first_half, second_half = (0, 1), (2, 3)
    ready(4)
    for a, b in zip(first_half, second_half):
        pass_on(0, 0, a, total(4, a))
        pass_on(1, 0, b, total(4, b))
    ready(3)
    ready(5)
    for a, b in zip(second_half, first_half):
        pass_on(0, 1, a, total(3, a))
        pass_on(1, 1, b, total(5, b))
    for a, b in zip(first_half, second_half):
        pass_on(0, 1, a, total(3, a) + came(0, 0, a))
        pass_on(1, 1, b, total(5, b) + came(1, 0, b))
    ready(2)
    ready(6)
    for a, b in zip(second_half + first_half, first_half + second_half):
        pass_on(0, 2, a, total(2, a) + came(0, 1, a))
        pass_on(1, 2, b, total(6, b) + came(1, 1, b))
    ready(1)
    ready(7)
    ready(0)

    def finish(i, d, p, value):
        here = last_vm.at[i, p]
        here[...] = value.astype(BF16)
        there = final_vm.at[i, r]
        copy = remote(here, there, last_send.at[i, p], last_recv.at[i, r], device(dp, z + d, p))
        if d:
            copy.start()
            sends.append(copy)
        else:
            @pl.when(p != r)
            def _():
                copy.start()

            @pl.when(p == r)
            def _():
                there[...] = here[...]

    for p in range(QUAD):
        finish(2, 0, p, total(0, p))
    for a, b in zip(second_half + first_half, first_half + second_half):
        finish(0, 1, a, total(1, a) + came(0, 2, a))
        finish(1, -1, b, total(7, b) + came(1, 2, b))
    for t in range(QUAD):
        for i in range(3):
            here = final_vm.at[i, t]
            arrival = remote(here, here, last_send.at[i, t], last_recv.at[i, t], device(dp, z, r ^ 1))
            if i < 2:
                arrival.wait_recv()
            else:
                @pl.when(t != r)
                def _():
                    arrival.wait_recv()
        value = final_vm[0, t].astype(F32) + final_vm[1, t].astype(F32) + final_vm[2, t].astype(F32)
        out = vgrad_ref if t % 2 else kgrad_ref
        out[:, (t // 2) * HD : (t // 2 + 1) * HD] = value.astype(BF16)
    for p in range(QUAD):
        @pl.when(p != r)
        def _():
            here = last_vm.at[2, p]
            remote(here, here, last_send.at[2, p], last_recv.at[2, p], device(dp, z, r ^ 1)).wait_send()
    for copy in sends:
        copy.wait_send()
    for d in order:
        crossings[d].wait_send()
    for copy in heads:
        copy.wait()


ANY = pl.BlockSpec(memory_space=pl.ANY)
VMEM = pl.BlockSpec(memory_space=pltpu.VMEM)
SMEM = pl.BlockSpec(memory_space=pltpu.SMEM)
DMA = pltpu.SemaphoreType.DMA


def gather(query, keys, values, attn_out, grad_out, log_total):
    return pl.pallas_call(
        gather_kernel,
        out_shape=(
            jax.ShapeDtypeStruct((SHARD, COLS), BF16),
            jax.ShapeDtypeStruct((SHARD, COLS), BF16),
            jax.ShapeDtypeStruct((2, SEQ, HD), BF16),
            jax.ShapeDtypeStruct((QUAD, 2, 2, QUAD, MEMBER_HEADS * HALF), F32),
        ),
        in_specs=[ANY] * 5 + [VMEM],
        out_specs=(ANY, ANY, ANY, ANY),
        scratch_shapes=[
            pltpu.VMEM((ROWS, HEADS * HD), BF16),
            pltpu.VMEM((ROWS, HEADS * HD), BF16),
            pltpu.VMEM((2, 2, QUAD, MEMBER_HEADS * HALF), F32),
            DMA((2,)),
            DMA((3, QUAD)),
            DMA,
            DMA((RING, QUAD)),
            DMA((RING, QUAD)),
            DMA((2, RING, QUAD)),
            DMA((RING, QUAD)),
            DMA((3, QUAD)),
            DMA((3, QUAD)),
            DMA((3,)),
        ],
        compiler_params=pltpu.CompilerParams(
            collective_id=0, has_side_effects=True, vmem_limit_bytes=24 * 2**20
        ),
    )(query, keys, values, attn_out, grad_out, log_total)


def attend(doc_lengths, block_order, q, do, kv, ld):
    return pl.pallas_call(
        attend_kernel,
        out_shape=(
            jax.ShapeDtypeStruct((SHARD, COLS), BF16),
            jax.ShapeDtypeStruct((2, SEQ, HD), BF16),
        ),
        in_specs=[SMEM, SMEM, VMEM, VMEM, VMEM, VMEM],
        out_specs=(VMEM, VMEM),
        scratch_shapes=[
            pltpu.VMEM((2, SEQ, HD), F32),
            pltpu.VMEM((HD, MEMBER_HEADS * HALF), F32),
            pltpu.SMEM((SEQ // HALF,), jnp.int32),
        ],
        compiler_params=pltpu.CompilerParams(vmem_limit_bytes=40 * 2**20),
    )(doc_lengths, block_order, q, do, kv, ld)


def reduce(dq, dkv):
    return pl.pallas_call(
        reduce_kernel,
        out_shape=(
            jax.ShapeDtypeStruct((ROWS, HEADS * HD), BF16),
            jax.ShapeDtypeStruct((ROWS, GROUPS * HD), BF16),
            jax.ShapeDtypeStruct((ROWS, GROUPS * HD), BF16),
        ),
        in_specs=[ANY, ANY],
        out_specs=(ANY, VMEM, VMEM),
        scratch_shapes=[
            pltpu.VMEM((SEQ, HD), BF16),
            pltpu.VMEM((SEQ, HD), BF16),
            pltpu.VMEM((2, 3, QUAD, ROWS, HD), BF16),
            pltpu.VMEM((2, 3, QUAD, ROWS, HD), BF16),
            pltpu.VMEM((3, QUAD, ROWS, HD), BF16),
            pltpu.VMEM((3, QUAD, ROWS, HD), BF16),
            DMA((RING,)),
            DMA((RING,)),
            DMA((RING,)),
            DMA((2, 3, QUAD)),
            DMA((2, 3, QUAD)),
            DMA((3, QUAD)),
            DMA((3, QUAD)),
            DMA((QUAD,)),
            DMA((QUAD,)),
            DMA,
        ],
        compiler_params=pltpu.CompilerParams(
            collective_id=1, has_side_effects=True, vmem_limit_bytes=24 * 2**20
        ),
    )(dq, dkv)


def local(query, keys, values, attn_out, grad_out, log_total, doc_lengths, block_order):
    q, do, kv, ld = gather(query, keys, values, attn_out, grad_out, log_total)
    dq, dkv = attend(doc_lengths, block_order, q, do, kv, ld)
    return reduce(dq, dkv)


def solution(mesh):
    rows = P(("dp", "ctx"), None)
    return jax.shard_map(
        local,
        mesh=mesh,
        in_specs=(rows, rows, rows, rows, rows, P(None, ("dp", "ctx")), P("dp"), P("dp")),
        out_specs=(rows, rows, rows),
        check_vma=False,
    )
```

```python
import functools

import jax
import jax.numpy as jnp
from jax import lax
from jax.experimental import pallas as pl
from jax.experimental.pallas import tpu as pltpu
from jax.sharding import PartitionSpec as P

HD = 128
HEADS = 16
GROUPS = 2
HALF = 64
ROWS = 128
QUAD = 4
RING = 8
SEQ = ROWS * QUAD * RING
SHARD = ROWS * QUAD
COLS = HEADS * HD // QUAD
MEMBER_HEADS = HEADS // QUAD
WINDOW = 1024 // HALF + 1
TILES = ((0, WINDOW),)
NDOC = 16
BLOCKS = SEQ // HALF
BLOCKS_HERE = SHARD // HALF
LANES = MEMBER_HEADS * HALF
MESH = pl.DeviceIdType.MESH
INV_ROOT = HD ** (-0.5)
LOG2E = 1.4426950408889634
F32 = jnp.float32
BF16 = jnp.bfloat16


def place():
    me = lax.axis_index("ctx")
    return lax.axis_index("dp"), me // QUAD, lax.rem(me, QUAD)


def device(dp, z, member):
    return (dp, lax.rem(z + RING, RING) * QUAD + member)


def greet(dp, z, r):
    barrier = pltpu.get_barrier_semaphore()
    for dz in (1, -1):
        for t in range(QUAD):
            pl.semaphore_signal(barrier, inc=1, device_id=device(dp, z + dz, t), device_id_type=MESH)
    for other in range(1, QUAD):
        pl.semaphore_signal(barrier, inc=1, device_id=device(dp, z, r ^ other), device_id_type=MESH)
    return lambda: pl.semaphore_wait(barrier, 2 * QUAD + QUAD - 1)


def rows_at(start, count):
    return pl.ds(pl.multiple_of(start, count), count)


def remote(src, dst, send_sem, recv_sem, target):
    return pltpu.make_async_remote_copy(
        src_ref=src, dst_ref=dst, send_sem=send_sem, recv_sem=recv_sem, device_id=target, device_id_type=MESH
    )


def split_lanes(table, half):
    pieces = []
    for t in range(QUAD):
        heads = [
            table[t * MEMBER_HEADS + e : t * MEMBER_HEADS + e + 1, half * HALF : (half + 1) * HALF]
            for e in range(MEMBER_HEADS)
        ]
        pieces.append(jnp.concatenate(heads, axis=1))
    return jnp.concatenate(pieces, axis=0)


def dot_tt(a, b):
    return lax.dot_general(a, b, (((1,), (1,)), ((), ())), preferred_element_type=F32)


def attend(z, r, qg_ref, dog_ref, kv_ref, ld_ref, order_sm, slot_sm, begin_vm, part_vm, dq_ref):
    @pl.loop(0, BLOCKS_HERE)
    def _(block):
        b = order_sm[z * BLOCKS_HERE + block]
        tok_q = b * HALF + lax.broadcasted_iota(jnp.int32, (1, LANES), 1) % HALF
        begin_q = begin_vm[block]
        rows = rows_at(block * HALF, HALF)
        q = jnp.concatenate([qg_ref[rows, e * HD : (e + 1) * HD] for e in range(MEMBER_HEADS)], axis=0)
        do = jnp.concatenate([dog_ref[rows, e * HD : (e + 1) * HD] for e in range(MEMBER_HEADS)], axis=0)
        lse = ld_ref[block // 2, 0, lax.rem(block, 2), pl.ds(r, 1), :]
        delta = ld_ref[block // 2, 1, lax.rem(block, 2), pl.ds(r, 1), :]
        dqt = jnp.zeros((HD, LANES), F32)
        for first, last in TILES:
            base = b - (WINDOW - 1) + first
            places = [slot_sm[block, j] for j in range(first, last)]
            k = jnp.concatenate([kv_ref[0, place] for place in places], axis=0)
            v = jnp.concatenate([kv_ref[1, place] for place in places], axis=0)
            tok_k = base * HALF + lax.broadcasted_iota(jnp.int32, ((last - first) * HALF, 1), 0)
            visible = (tok_k <= tok_q) & (tok_k >= begin_q)
            score = dot_tt(k, q)
            probs = jnp.exp2(jnp.where(visible, score * (INV_ROOT * LOG2E) - lse, -1e30))
            dprobs = dot_tt(v, do)
            dscore = (probs * (dprobs - delta)).astype(BF16)
            probs_low = probs.astype(BF16)
            there = slice(first + 1, last + 1)
            blocks = (last - first, HALF, HD)
            part_vm[1, block, there] = jnp.dot(probs_low, do, preferred_element_type=F32).reshape(blocks)
            part_vm[0, block, there] = jnp.dot(dscore, q, preferred_element_type=F32).reshape(blocks)
            dqt += lax.dot_general(k, dscore, (((0,), (0,)), ((), ())), preferred_element_type=F32)
        dq = (dqt.T * INV_ROOT).astype(BF16)
        for e in range(MEMBER_HEADS):
            dq_ref[rows, e * HD : (e + 1) * HD] = dq[e * HALF : (e + 1) * HALF]


def kernel(
    q_ref, k_ref, v_ref, o_ref, do_ref, lse_ref, doc_ref, order_ref,
    qgrad_ref, kgrad_ref, vgrad_ref,
    o_vm, do_vm, own_kv, lse_vm, ld_vm, qg_ref, dog_ref, kv_ref, ld_ref,
    doc_sm, order_sm, slot_vm, slot_sm, begin_vm, part_vm, dq_ref,
    own_vm, give_vm, other_vm, recv_vm, send_vm, last_vm, final_vm,
    load_sem, own_sem, first_send, first_own, own_recv, other_recv, ring_send, core_send, head_send, head_recv, head_own,
    give_send, give_recv, sum_send, sum_recv, last_send, last_recv, back_send, back_recv, back_own,
):
    dp, z, r = place()
    core = lax.rem(r, 2)
    greeted = greet(dp, z, r)
    loads = [
        pltpu.make_async_copy(o_ref, o_vm, load_sem.at[0]),
        pltpu.make_async_copy(do_ref, do_vm, load_sem.at[1]),
        pltpu.make_async_copy(lse_ref, lse_vm, load_sem.at[2]),
        pltpu.make_async_copy(doc_ref, doc_sm, load_sem.at[3]),
        pltpu.make_async_copy(order_ref, order_sm, load_sem.at[4]),
    ]
    own = []
    for i, (source, kind, g, half) in enumerate(
        (ref, kind, g, half) for kind, ref in ((0, k_ref), (1, v_ref)) for g in range(GROUPS) for half in range(2)
    ):
        block = source.at[half * HALF : (half + 1) * HALF, g * HD : (g + 1) * HD]
        own.append(pltpu.make_async_copy(block, own_kv.at[kind, g, half], own_sem.at[i]))
    for c in own + loads:
        c.start()
    for c in loads[:3]:
        c.wait()
    prod = do_vm[...].astype(F32) * o_vm[...].astype(F32)
    high = prod.astype(BF16)
    low = (prod - high.astype(F32)).astype(BF16)
    head_of = lax.broadcasted_iota(jnp.int32, (HEADS, HEADS * HD), 1) // HD
    ones = (head_of == lax.broadcasted_iota(jnp.int32, (HEADS, HEADS * HD), 0)).astype(BF16)
    along = (((1,), (1,)), ((), ()))
    delta = lax.dot_general(ones, high, along, preferred_element_type=F32) + lax.dot_general(
        ones, low, along, preferred_element_type=F32
    )
    for half in range(2):
        ld_vm[0, half] = split_lanes(lse_vm[...] * LOG2E, half)
        ld_vm[1, half] = split_lanes(delta, half)
    for c in own:
        c.wait()
    greeted()

    def kv_rows(shard, member):
        return pl.ds((lax.rem(shard + RING, RING) * QUAD + member) * 2, 2)

    first = []
    mine = kv_rows(z, r)
    for i, dz in enumerate((1, -1, 0)):
        for t in range(QUAD):
            source = own_kv.at[t % 2, t // 2]
            target = kv_ref.at[t % 2, mine]
            copy = remote(source, target, first_send.at[i, t], own_recv.at[dz % RING, r], device(dp, z + dz, t))
            if dz:
                copy.start()
                first.append(copy)
            else:
                @pl.when(t != r)
                def _():
                    copy.start()

                @pl.when(t == r)
                def _():
                    pltpu.make_async_copy(source, target, first_own).start()

    heads = []
    for i, (src, dst) in enumerate(((q_ref, qg_ref), (do_ref, dog_ref))):
        to_rows = rows_at(r * ROWS, ROWS)
        for other in range(1, QUAD):
            t = r ^ other
            cols = rows_at(t * COLS, COLS)
            copy = remote(
                src.at[:, cols], dst.at[to_rows, :], head_send.at[i, other], head_recv.at[i, other], device(dp, z, t)
            )
            copy.start()
            heads.append(copy)
        own = pltpu.make_async_copy(src.at[:, rows_at(r * COLS, COLS)], dst.at[to_rows, :], head_own.at[i])
        own.start()
        heads.append(own)

    for other in range(1, QUAD):
        copy = remote(ld_vm, ld_ref.at[r], head_send.at[2, other], head_recv.at[2, other], device(dp, z, r ^ other))
        copy.start()
        heads.append(copy)
    own = pltpu.make_async_copy(ld_vm, ld_ref.at[r], head_own.at[2])
    own.start()
    heads.append(own)

    forwards = []
    crossings = []

    def slot(k, p):
        return kv_ref.at[core, kv_rows(z - k, p)]

    def arrived(k, p):
        piece = slot(k, p)
        remote(piece, piece, first_send.at[0, 0], own_recv.at[k, p], device(dp, z, r ^ 1)).wait_recv()
        return piece

    def forward(k, p, step, piece):
        i = 0 if step > 0 else 1
        copy = remote(piece, piece, ring_send.at[i, k, p], own_recv.at[k + step, p], device(dp, z + step, r))
        copy.start()
        forwards.append(copy)

    def cross(k, p, piece):
        copy = remote(piece, piece, core_send.at[k, p], other_recv.at[k, p], device(dp, z, r ^ 1))
        copy.start()
        crossings.append((copy, k, p))

    for k in range(1, 4):
        for p in range(QUAD):
            piece = arrived(k, p)
            if k < 3 or p < 2:
                forward(k, p, 1, piece)
            cross(k, p, piece)
            piece = arrived(RING - k, p)
            if k < 3 or p >= 2:
                forward(RING - k, p, -1, piece)
            cross(RING - k, p, piece)
        if k == 1:
            for c in loads[3:]:
                c.wait()
            wanted = jnp.concatenate(
                [jnp.full((1, HD), order_sm[z * BLOCKS_HERE + block], jnp.int32) for block in range(BLOCKS_HERE)], axis=0
            )
            wanted = wanted - (WINDOW - 1) + lax.broadcasted_iota(jnp.int32, (BLOCKS_HERE, HD), 1)
            slots = lax.fori_loop(
                0, BLOCKS, lambda i, found: jnp.where(wanted == order_sm[i], i, found), jnp.zeros_like(wanted)
            )
            slot_vm[...] = slots
            to_scalars = pltpu.make_async_copy(slot_vm, slot_sm, load_sem.at[5])
            to_scalars.start()
            for p in range(QUAD):
                piece = slot(0, p)

                @pl.when(p != r)
                def _():
                    arrived(0, p)

                @pl.when(p == r)
                def _():
                    pltpu.make_async_copy(piece, piece, first_own).wait()

                cross(0, p, piece)
        if k == 2:
            within = lax.broadcasted_iota(jnp.int32, (1, LANES), 1) % HALF

            @pl.loop(0, BLOCKS_HERE)
            def _(block):
                tok_q = order_sm[z * BLOCKS_HERE + block] * HALF + within
                begin_q = jnp.zeros((1, LANES), jnp.int32)
                end = jnp.int32(0)
                for d in range(NDOC):
                    end = end + doc_sm[d]
                    begin_q = jnp.where(end <= tok_q, end, begin_q)
                begin_vm[block] = begin_q
                for kind in range(2):
                    part_vm[kind, block, 0] = jnp.zeros((HALF, HD), F32)
                    part_vm[kind, block, WINDOW + 1] = jnp.zeros((HALF, HD), F32)
    to_scalars.wait()
    for p in range(QUAD):
        cross(4, p, arrived(4, p))
    for copy, k, p in crossings:
        copy.wait_send()
        theirs = kv_ref.at[1 - core, kv_rows(z - k, p)]
        remote(theirs, theirs, core_send.at[k, p], other_recv.at[k, p], device(dp, z, r ^ 1)).wait_recv()
    for copy in heads:
        copy.wait()
    attend(z, r, qg_ref, dog_ref, kv_ref, ld_ref, order_sm, slot_sm, begin_vm, part_vm, dq_ref)
    for copy in forwards + first:
        copy.wait_send()
    for t in range(QUAD):
        @pl.when(t != r)
        def _():
            piece = slot(0, 0)
            remote(piece, piece, first_send.at[2, t], own_recv.at[0, 0], device(dp, z, r ^ 1)).wait_send()


    def shard(d):
        return rows_at(lax.rem(z + d + RING, RING) * SHARD, SHARD)

    def piece(d, p):
        return rows_at((lax.rem(z + d + RING, RING) * QUAD + p) * ROWS, ROWS)

    order = (4, 3, 5, 2, 6, 1, 7, 0)
    gifts = {}

    def combine(d):
        start = lax.rem(z + d + RING, RING) * BLOCKS_HERE

        @pl.loop(0, BLOCKS_HERE)
        def _(i):
            kb = order_sm[start + i]
            places = []
            for block in range(BLOCKS_HERE):
                at = kb - order_sm[z * BLOCKS_HERE + block] + (WINDOW - 1)
                places.append(jnp.clip(at + 1, 0, WINDOW + 1))
            rows = rows_at((start + i) * HALF, HALF)
            for out, kind in ((give_vm, 1 - core), (own_vm, core)):
                terms = [part_vm[kind, block, places[block]] for block in range(BLOCKS_HERE)]
                while len(terms) > 1:
                    terms = [x + y for x, y in zip(terms[::2], terms[1::2])]
                out[rows, :] = (terms[0] * jnp.where(kind == 0, INV_ROOT, 1.0)).astype(out.dtype)

        gifts[d] = remote(
            give_vm.at[shard(d), :], other_vm.at[shard(d), :], give_send.at[d], give_recv.at[d], device(dp, z, r ^ 1)
        )
        gifts[d].start()

    heads = []
    combine(4)
    to_cols = rows_at(r * COLS, COLS)
    for other in range(1, QUAD):
        t = r ^ other
        copy = remote(
            dq_ref.at[rows_at(t * ROWS, ROWS), :], qgrad_ref.at[:, to_cols],
            back_send.at[other], back_recv.at[other], device(dp, z, t),
        )
        copy.start()
        heads.append(copy)
    own = pltpu.make_async_copy(dq_ref.at[rows_at(r * ROWS, ROWS), :], qgrad_ref.at[:, to_cols], back_own)
    own.start()
    heads.append(own)

    def total(d, p):
        return own_vm[piece(d, p), :] + other_vm[piece(d, p), :].astype(F32)

    def ready(d):
        gifts[d].wait_recv()

    sends = []

    def pass_on(i, s, p, value):
        here = send_vm.at[i, s, p]
        here[...] = value.astype(BF16)
        copy = remote(
            here, recv_vm.at[i, s, p], sum_send.at[i, s, p], sum_recv.at[i, s, p],
            device(dp, z + (1 - 2 * i), r),
        )
        copy.start()
        sends.append(copy)

    def came(i, s, p):
        here = recv_vm.at[i, s, p]
        remote(here, here, sum_send.at[i, s, p], sum_recv.at[i, s, p], device(dp, z, r ^ 1)).wait_recv()
        return here[...].astype(F32)

    first_half, second_half = (0, 1), (2, 3)
    combine(3)
    combine(5)
    ready(4)
    for a, b in zip(first_half, second_half):
        pass_on(0, 0, a, total(4, a))
        pass_on(1, 0, b, total(4, b))
    ready(3)
    ready(5)
    for a, b in zip(second_half, first_half):
        pass_on(0, 1, a, total(3, a))
        pass_on(1, 1, b, total(5, b))
    combine(2)
    combine(6)
    for a, b in zip(first_half, second_half):
        pass_on(0, 1, a, total(3, a) + came(0, 0, a))
        pass_on(1, 1, b, total(5, b) + came(1, 0, b))
    combine(1)
    combine(7)
    combine(0)
    ready(2)
    ready(6)
    for a, b in zip(second_half + first_half, first_half + second_half):
        pass_on(0, 2, a, total(2, a) + came(0, 1, a))
        pass_on(1, 2, b, total(6, b) + came(1, 1, b))
    ready(1)
    ready(7)
    ready(0)

    def finish(i, d, p, value):
        here = last_vm.at[i, p]
        here[...] = value.astype(BF16)
        there = final_vm.at[i, r]
        copy = remote(here, there, last_send.at[i, p], last_recv.at[i, r], device(dp, z + d, p))
        if d:
            copy.start()
            sends.append(copy)
        else:
            @pl.when(p != r)
            def _():
                copy.start()

            @pl.when(p == r)
            def _():
                there[...] = here[...]

    for p in range(QUAD):
        finish(2, 0, p, total(0, p))
    for a, b in zip(second_half + first_half, first_half + second_half):
        finish(0, 1, a, total(1, a) + came(0, 2, a))
        finish(1, -1, b, total(7, b) + came(1, 2, b))
    for t in range(QUAD):
        for i in range(3):
            here = final_vm.at[i, t]
            arrival = remote(here, here, last_send.at[i, t], last_recv.at[i, t], device(dp, z, r ^ 1))
            if i < 2:
                arrival.wait_recv()
            else:
                @pl.when(t != r)
                def _():
                    arrival.wait_recv()
        value = final_vm[0, t].astype(F32) + final_vm[1, t].astype(F32) + final_vm[2, t].astype(F32)
        out = vgrad_ref if t % 2 else kgrad_ref
        out[:, (t // 2) * HD : (t // 2 + 1) * HD] = value.astype(BF16)
    for p in range(QUAD):
        @pl.when(p != r)
        def _():
            here = last_vm.at[2, p]
            remote(here, here, last_send.at[2, p], last_recv.at[2, p], device(dp, z, r ^ 1)).wait_send()
    for copy in sends:
        copy.wait_send()
    for d in order:
        gifts[d].wait_send()
    for copy in heads:
        copy.wait()


ANY = pl.BlockSpec(memory_space=pl.ANY)
VMEM = pl.BlockSpec(memory_space=pltpu.VMEM)
DMA = pltpu.SemaphoreType.DMA
LIMIT = 60


def local(query, keys, values, attn_out, grad_out, log_total, doc_lengths, block_order):
    return pl.pallas_call(
        kernel,
        out_shape=(
            jax.ShapeDtypeStruct((ROWS, HEADS * HD), BF16),
            jax.ShapeDtypeStruct((ROWS, GROUPS * HD), BF16),
            jax.ShapeDtypeStruct((ROWS, GROUPS * HD), BF16),
        ),
        in_specs=[ANY] * 8,
        out_specs=(ANY, VMEM, VMEM),
        scratch_shapes=[
            pltpu.VMEM((ROWS, HEADS * HD), BF16),
            pltpu.VMEM((ROWS, HEADS * HD), BF16),
            pltpu.VMEM((2, GROUPS, 2, HALF, HD), BF16),
            pltpu.VMEM((HEADS, ROWS), F32),
            pltpu.VMEM((2, 2, QUAD, LANES), F32),
            pltpu.VMEM((SHARD, COLS), BF16),
            pltpu.VMEM((SHARD, COLS), BF16),
            pltpu.VMEM((2, BLOCKS, HALF, HD), BF16),
            pltpu.VMEM((QUAD, 2, 2, QUAD, LANES), F32),
            pltpu.SMEM((NDOC,), jnp.int32),
            pltpu.SMEM((BLOCKS,), jnp.int32),
            pltpu.VMEM((BLOCKS_HERE, HD), jnp.int32),
            pltpu.SMEM((BLOCKS_HERE, HD), jnp.int32),
            pltpu.VMEM((BLOCKS_HERE, 1, LANES), jnp.int32),
            pltpu.VMEM((2, BLOCKS_HERE, WINDOW + 2, HALF, HD), F32),
            pltpu.VMEM((SHARD, COLS), BF16),
            pltpu.VMEM((SEQ, HD), F32),
            pltpu.VMEM((SEQ, HD), BF16),
            pltpu.VMEM((SEQ, HD), BF16),
            pltpu.VMEM((2, 3, QUAD, ROWS, HD), BF16),
            pltpu.VMEM((2, 3, QUAD, ROWS, HD), BF16),
            pltpu.VMEM((3, QUAD, ROWS, HD), BF16),
            pltpu.VMEM((3, QUAD, ROWS, HD), BF16),
            DMA((6,)),
            DMA((8,)),
            DMA((3, QUAD)),
            DMA,
            DMA((RING, QUAD)),
            DMA((RING, QUAD)),
            DMA((2, RING, QUAD)),
            DMA((RING, QUAD)),
            DMA((3, QUAD)),
            DMA((3, QUAD)),
            DMA((3,)),
            DMA((RING,)),
            DMA((RING,)),
            DMA((2, 3, QUAD)),
            DMA((2, 3, QUAD)),
            DMA((3, QUAD)),
            DMA((3, QUAD)),
            DMA((QUAD,)),
            DMA((QUAD,)),
            DMA,
        ],
        compiler_params=pltpu.CompilerParams(
            collective_id=0, has_side_effects=True, vmem_limit_bytes=LIMIT * 2**20
        ),
    )(query, keys, values, attn_out, grad_out, log_total, doc_lengths, block_order)


def solution(mesh):
    rows = P(("dp", "ctx"), None)
    return jax.shard_map(
        local,
        mesh=mesh,
        in_specs=(rows, rows, rows, rows, rows, P(None, ("dp", "ctx")), P("dp"), P("dp")),
        out_specs=(rows, rows, rows),
        check_vma=False,
    )
```

```python
import functools

import jax
import jax.numpy as jnp
from jax import lax
from jax.experimental import pallas as pl
from jax.experimental.pallas import tpu as pltpu
from jax.sharding import PartitionSpec as P

HD = 128
HEADS = 16
GROUPS = 2
HALF = 64
ROWS = 128
QUAD = 4
RING = 8
SEQ = ROWS * QUAD * RING
SHARD = ROWS * QUAD
COLS = HEADS * HD // QUAD
MEMBER_HEADS = HEADS // QUAD
WINDOW = 1024 // HALF + 1
TILES = ((0, WINDOW),)
NDOC = 16
BLOCKS = SEQ // HALF
BLOCKS_HERE = SHARD // HALF
LANES = MEMBER_HEADS * HALF
MESH = pl.DeviceIdType.MESH
INV_ROOT = HD ** (-0.5)
LOG2E = 1.4426950408889634
F32 = jnp.float32
BF16 = jnp.bfloat16


def place():
    me = lax.axis_index("ctx")
    return lax.axis_index("dp"), me // QUAD, lax.rem(me, QUAD)


def device(dp, z, member):
    return (dp, lax.rem(z + RING, RING) * QUAD + member)


def greet(dp, z, r):
    barrier = pltpu.get_barrier_semaphore()
    for dz in (1, -1):
        for t in range(QUAD):
            pl.semaphore_signal(barrier, inc=1, device_id=device(dp, z + dz, t), device_id_type=MESH)
    for other in range(1, QUAD):
        pl.semaphore_signal(barrier, inc=1, device_id=device(dp, z, r ^ other), device_id_type=MESH)
    return lambda: pl.semaphore_wait(barrier, 2 * QUAD + QUAD - 1)


def rows_at(start, count):
    return pl.ds(pl.multiple_of(start, count), count)


def remote(src, dst, send_sem, recv_sem, target):
    return pltpu.make_async_remote_copy(
        src_ref=src, dst_ref=dst, send_sem=send_sem, recv_sem=recv_sem, device_id=target, device_id_type=MESH
    )


def split_lanes(table, half):
    pieces = []
    for t in range(QUAD):
        heads = [
            table[t * MEMBER_HEADS + e : t * MEMBER_HEADS + e + 1, half * HALF : (half + 1) * HALF]
            for e in range(MEMBER_HEADS)
        ]
        pieces.append(jnp.concatenate(heads, axis=1))
    return jnp.concatenate(pieces, axis=0)


def dot_tt(a, b):
    return lax.dot_general(a, b, (((1,), (1,)), ((), ())), preferred_element_type=F32)


def attend(z, r, qg_ref, dog_ref, kv_ref, ld_ref, order_sm, slot_sm, begin_vm, part_vm, ds_vm, wait_far):
    @pl.loop(0, BLOCKS_HERE)
    def _(i):
        @pl.when(i == BLOCKS_HERE // 2)
        def _():
            wait_far()

        block = lax.rem(i + (r // 2) * (BLOCKS_HERE // 2), BLOCKS_HERE)
        b = order_sm[z * BLOCKS_HERE + block]
        tok_q = b * HALF + lax.broadcasted_iota(jnp.int32, (1, LANES), 1) % HALF
        begin_q = begin_vm[block]
        rows = rows_at(block * HALF, HALF)
        q = jnp.concatenate([qg_ref[rows, e * HD : (e + 1) * HD] for e in range(MEMBER_HEADS)], axis=0)
        do = jnp.concatenate([dog_ref[rows, e * HD : (e + 1) * HD] for e in range(MEMBER_HEADS)], axis=0)
        lse = ld_ref[block // 2, 0, lax.rem(block, 2), pl.ds(r, 1), :]
        delta = ld_ref[block // 2, 1, lax.rem(block, 2), pl.ds(r, 1), :]
        for first, last in TILES:
            base = b - (WINDOW - 1) + first
            places = [slot_sm[block, j] for j in range(first, last)]
            k = jnp.concatenate([kv_ref[0, place] for place in places], axis=0)
            v = jnp.concatenate([kv_ref[1, place] for place in places], axis=0)
            tok_k = base * HALF + lax.broadcasted_iota(jnp.int32, ((last - first) * HALF, 1), 0)
            visible = (tok_k <= tok_q) & (tok_k >= begin_q)
            score = dot_tt(k, q)
            probs = jnp.exp2(jnp.where(visible, score * (INV_ROOT * LOG2E) - lse, -1e30))
            dprobs = dot_tt(v, do)
            dscore = (probs * (dprobs - delta)).astype(BF16)
            probs_low = probs.astype(BF16)
            there = slice(first + 1, last + 1)
            blocks = (last - first, HALF, HD)
            part_vm[1, block, there] = jnp.dot(probs_low, do, preferred_element_type=F32).reshape(blocks)
            part_vm[0, block, there] = jnp.dot(dscore, q, preferred_element_type=F32).reshape(blocks)
            ds_vm[block, first * HALF : last * HALF, :] = dscore


def kernel(
    q_ref, k_ref, v_ref, o_ref, do_ref, lse_ref, doc_ref, order_ref,
    qgrad_ref, kgrad_ref, vgrad_ref,
    o_vm, do_vm, own_kv, lse_vm, ld_vm, qg_ref, dog_ref, kv_ref, ld_ref,
    doc_sm, order_sm, slot_vm, slot_sm, begin_vm, part_vm, ds_vm, dq_ref,
    own_vm, give_vm, other_vm, recv_vm, send_vm, last_vm, final_vm,
    load_sem, own_sem, first_send, first_own, first_recv, half_recv, other_recv, ring_send, core_send, head_send, head_recv, head_own,
    give_send, give_recv, sum_send, sum_recv, last_send, last_recv, back_send, back_recv, back_own,
):
    dp, z, r = place()
    core = lax.rem(r, 2)
    greeted = greet(dp, z, r)
    loads = [
        pltpu.make_async_copy(o_ref, o_vm, load_sem.at[0]),
        pltpu.make_async_copy(do_ref, do_vm, load_sem.at[1]),
        pltpu.make_async_copy(lse_ref, lse_vm, load_sem.at[2]),
        pltpu.make_async_copy(doc_ref, doc_sm, load_sem.at[3]),
        pltpu.make_async_copy(order_ref, order_sm, load_sem.at[4]),
    ]
    own = []
    for i, (source, kind, g, half) in enumerate(
        (ref, kind, g, half) for kind, ref in ((0, k_ref), (1, v_ref)) for g in range(GROUPS) for half in range(2)
    ):
        block = source.at[half * HALF : (half + 1) * HALF, g * HD : (g + 1) * HD]
        own.append(pltpu.make_async_copy(block, own_kv.at[kind, g, half], own_sem.at[i]))
    for c in own + loads:
        c.start()
    for c in loads[:3]:
        c.wait()
    prod = do_vm[...].astype(F32) * o_vm[...].astype(F32)
    high = prod.astype(BF16)
    low = (prod - high.astype(F32)).astype(BF16)
    head_of = lax.broadcasted_iota(jnp.int32, (HEADS, HEADS * HD), 1) // HD
    ones = (head_of == lax.broadcasted_iota(jnp.int32, (HEADS, HEADS * HD), 0)).astype(BF16)
    along = (((1,), (1,)), ((), ()))
    delta = lax.dot_general(ones, high, along, preferred_element_type=F32) + lax.dot_general(
        ones, low, along, preferred_element_type=F32
    )
    for half in range(2):
        ld_vm[0, half] = split_lanes(lse_vm[...] * LOG2E, half)
        ld_vm[1, half] = split_lanes(delta, half)
    for c in own:
        c.wait()
    greeted()

    def kv_rows(shard, member):
        return pl.ds((lax.rem(shard + RING, RING) * QUAD + member) * 2, 2)

    first = []
    mine = kv_rows(z, r)
    for i, dz in enumerate((1, -1, 0)):
        for t in range(QUAD):
            source = own_kv.at[t % 2, t // 2]
            target = kv_ref.at[t % 2, mine]
            copy = remote(source, target, first_send.at[i, t], first_recv.at[i, r], device(dp, z + dz, t))
            if i != 2:
                copy.start()
                first.append(copy)
            else:
                @pl.when(t != r)
                def _():
                    copy.start()

                @pl.when(t == r)
                def _():
                    pltpu.make_async_copy(source, target, first_own).start()

    near_heads = []
    far_heads = []
    for i, (src, dst) in enumerate(((q_ref, qg_ref), (do_ref, dog_ref))):
        to_rows = rows_at(r * ROWS, ROWS)
        for other in range(1, QUAD):
            t = r ^ other
            cols = rows_at(t * COLS, COLS)
            copy = remote(
                src.at[:, cols], dst.at[to_rows, :], head_send.at[i, other], head_recv.at[i, other], device(dp, z, t)
            )
            copy.start()
            (near_heads if other == 1 else far_heads).append(copy)
        own = pltpu.make_async_copy(src.at[:, rows_at(r * COLS, COLS)], dst.at[to_rows, :], head_own.at[i])
        own.start()
        near_heads.append(own)

    for other in range(1, QUAD):
        copy = remote(ld_vm, ld_ref.at[r], head_send.at[2, other], head_recv.at[2, other], device(dp, z, r ^ other))
        copy.start()
        (near_heads if other == 1 else far_heads).append(copy)
    own = pltpu.make_async_copy(ld_vm, ld_ref.at[r], head_own.at[2])
    own.start()
    near_heads.append(own)

    forwards = []
    crossings = []

    def half_of(k, h):
        return kv_ref.at[core, pl.ds((lax.rem(z - k + RING, RING) * 2 + h) * QUAD, QUAD)]

    def first_arrived(i, pieces):
        for p in pieces:
            there = kv_ref.at[core, kv_rows(z, p)]
            arrival = remote(there, there, first_send.at[i, 0], first_recv.at[i, p], device(dp, z, r ^ 1))
            if i < 2:
                arrival.wait_recv()
            else:
                @pl.when(p != r)
                def _():
                    arrival.wait_recv()

                @pl.when(p == r)
                def _():
                    pltpu.make_async_copy(there, there, first_own).wait()

    def arrived(k, h):
        there = half_of(k, h)
        remote(there, there, ring_send.at[0, k, h], half_recv.at[k, h], device(dp, z, r ^ 1)).wait_recv()

    def forward(i, k, h):
        step = 1 - 2 * i
        there = half_of(k, h)
        copy = remote(there, there, ring_send.at[i, k, h], half_recv.at[k + step, h], device(dp, z + step, r))
        copy.start()
        forwards.append(copy)

    def crossed(kind, k, h=None):
        zk = lax.rem(z - k + RING, RING)
        if h is None:
            there = kv_ref.at[kind, pl.ds(zk * BLOCKS_HERE, BLOCKS_HERE)]
        else:
            there = kv_ref.at[kind, pl.ds((zk * 2 + h) * QUAD, QUAD)]
        at = k if not h else RING
        return remote(there, there, core_send.at[at], other_recv.at[at], device(dp, z, r ^ 1))

    def cross(k, h=None):
        copy = crossed(core, k, h)
        copy.start()
        crossings.append((copy, k, h))

    for h in range(2):
        for i, hi in ((0, h), (1, 1 - h)):
            first_arrived(i, (2 * hi, 2 * hi + 1))
            forward(i, 1 if i == 0 else RING - 1, hi)
    cross(1)
    cross(RING - 1)
    first_arrived(2, range(QUAD))
    cross(0)
    for c in loads[3:]:
        c.wait()
    wanted = jnp.concatenate(
        [jnp.full((1, HD), order_sm[z * BLOCKS_HERE + block], jnp.int32) for block in range(BLOCKS_HERE)], axis=0
    )
    wanted = wanted - (WINDOW - 1) + lax.broadcasted_iota(jnp.int32, (BLOCKS_HERE, HD), 1)
    slots = lax.fori_loop(
        0, BLOCKS, lambda i, found: jnp.where(wanted == order_sm[i], i, found), jnp.zeros_like(wanted)
    )
    slot_vm[...] = slots
    to_scalars = pltpu.make_async_copy(slot_vm, slot_sm, load_sem.at[5])
    to_scalars.start()
    for h in range(2):
        for i, k, hi in ((0, 2, h), (1, RING - 2, 1 - h)):
            arrived(k, hi)
            forward(i, k, hi)
    cross(2)
    cross(RING - 2)
    within = lax.broadcasted_iota(jnp.int32, (1, LANES), 1) % HALF

    @pl.loop(0, BLOCKS_HERE)
    def _(block):
        tok_q = order_sm[z * BLOCKS_HERE + block] * HALF + within
        begin_q = jnp.zeros((1, LANES), jnp.int32)
        end = jnp.int32(0)
        for d in range(NDOC):
            end = end + doc_sm[d]
            begin_q = jnp.where(end <= tok_q, end, begin_q)
        begin_vm[block] = begin_q
        for kind in range(2):
            part_vm[kind, block, 0] = jnp.zeros((HALF, HD), F32)
            part_vm[kind, block, WINDOW + 1] = jnp.zeros((HALF, HD), F32)
    to_scalars.wait()
    for h in range(2):
        for i, k, hi in ((0, 3, h), (1, RING - 3, 1 - h)):
            arrived(k, hi)
            if h == 0:
                forward(i, k, hi)
    cross(3)
    cross(RING - 3)
    for h in range(2):
        arrived(4, h)
        cross(4, h)
    for _, k, h in crossings:
        crossed(1 - core, k, h).wait_recv()
    for copy in near_heads:
        copy.wait()

    def wait_far_heads():
        for copy in far_heads:
            copy.wait()

    attend(z, r, qg_ref, dog_ref, kv_ref, ld_ref, order_sm, slot_sm, begin_vm, part_vm, ds_vm, wait_far_heads)
    def settle():
        for copy, _, _ in crossings:
            copy.wait_send()
        for copy in forwards + first:
            copy.wait_send()
        for t in range(QUAD):
            @pl.when(t != r)
            def _():
                there = kv_ref.at[0, kv_rows(z, 0)]
                remote(there, there, first_send.at[2, t], first_recv.at[2, 0], device(dp, z, r ^ 1)).wait_send()

    def shard(d):
        return rows_at(lax.rem(z + d + RING, RING) * SHARD, SHARD)

    def piece(d, p):
        return rows_at((lax.rem(z + d + RING, RING) * 2 + p) * ROWS * 2, ROWS * 2)

    order = (4, 3, 5, 2, 6, 1, 7, 0)
    gifts = {}

    def combine(d):
        start = lax.rem(z + d + RING, RING) * BLOCKS_HERE

        @pl.loop(0, BLOCKS_HERE)
        def _(i):
            kb = order_sm[start + i]
            places = []
            for block in range(BLOCKS_HERE):
                at = kb - order_sm[z * BLOCKS_HERE + block] + (WINDOW - 1)
                places.append(jnp.clip(at + 1, 0, WINDOW + 1))
            rows = rows_at((start + i) * HALF, HALF)
            for out, kind in ((give_vm, 1 - core), (own_vm, core)):
                terms = [part_vm[kind, block, places[block]] for block in range(BLOCKS_HERE)]
                while len(terms) > 1:
                    terms = [x + y for x, y in zip(terms[::2], terms[1::2])]
                out[rows, :] = (terms[0] * jnp.where(kind == 0, INV_ROOT, 1.0)).astype(out.dtype)

        gifts[d] = remote(
            give_vm.at[shard(d), :], other_vm.at[shard(d), :], give_send.at[d], give_recv.at[d], device(dp, z, r ^ 1)
        )
        gifts[d].start()

    heads = []
    to_cols = rows_at(r * COLS, COLS)

    def query_terms(first_member):
        @pl.loop(0, BLOCKS_HERE // 2)
        def _(i):
            block = first_member * 2 + i
            k = jnp.concatenate([kv_ref[0, slot_sm[block, j]] for j in range(WINDOW)], axis=0)
            dqt = lax.dot_general(k, ds_vm[block], (((0,), (0,)), ((), ())), preferred_element_type=F32)
            dq = (dqt.T * (INV_ROOT * 0.5)).astype(BF16)
            for e in range(MEMBER_HEADS):
                dq_ref[rows_at(block * HALF, HALF), e * HD : (e + 1) * HD] = dq[e * HALF : (e + 1) * HALF]

    def send_back(other):
        t = r ^ other
        copy = remote(
            dq_ref.at[rows_at(t * ROWS, ROWS), :], qgrad_ref.at[:, to_cols],
            back_send.at[other], back_recv.at[other], device(dp, z, t),
        )
        copy.start()
        heads.append(copy)

    def total(d, p):
        return own_vm[piece(d, p), :] + other_vm[piece(d, p), :].astype(F32)

    def ready(d):
        gifts[d].wait_recv()

    sends = []

    def pass_on(i, s, p, value):
        here = send_vm.at[i, s, p]
        here[...] = value.astype(BF16)
        copy = remote(
            here, recv_vm.at[i, s, p], sum_send.at[i, s, p], sum_recv.at[i, s, p],
            device(dp, z + (1 - 2 * i), r),
        )
        copy.start()
        sends.append(copy)

    def came(i, s, p):
        here = recv_vm.at[i, s, p]
        remote(here, here, sum_send.at[i, s, p], sum_recv.at[i, s, p], device(dp, z, r ^ 1)).wait_recv()
        return here[...].astype(F32)

    combine(4)
    combine(3)
    combine(5)
    ready(4)
    pass_on(0, 0, 0, total(4, 0))
    pass_on(1, 0, 1, total(4, 1))
    ready(3)
    ready(5)
    pass_on(0, 1, 1, total(3, 1))
    pass_on(1, 1, 0, total(5, 0))
    combine(2)
    combine(6)
    query_terms((1 - r // 2) * 2)
    send_back(2)
    send_back(3)
    pass_on(0, 1, 0, total(3, 0) + came(0, 0, 0))
    pass_on(1, 1, 1, total(5, 1) + came(1, 0, 1))
    ready(2)
    ready(6)
    for h in range(2):
        pass_on(0, 2, 1 - h, total(2, 1 - h) + came(0, 1, 1 - h))
        pass_on(1, 2, h, total(6, h) + came(1, 1, h))
    combine(1)
    combine(7)
    combine(0)
    query_terms((r // 2) * 2)
    send_back(1)
    own = pltpu.make_async_copy(dq_ref.at[rows_at(r * ROWS, ROWS), :], qgrad_ref.at[:, to_cols], back_own)
    own.start()
    heads.append(own)
    ready(1)
    ready(7)
    ready(0)

    def finish(i, d, h, value):
        for p in (2 * h, 2 * h + 1):
            here = last_vm.at[i, p]
            here[...] = value[(p - 2 * h) * ROWS : (p - 2 * h + 1) * ROWS].astype(BF16)
            there = final_vm.at[i, r]
            copy = remote(here, there, last_send.at[i, p], last_recv.at[i, r], device(dp, z + d, p))
            if d:
                copy.start()
                sends.append(copy)
            else:
                @pl.when(p != r)
                def _():
                    copy.start()

                @pl.when(p == r)
                def _():
                    there[...] = here[...]

    for h in range(2):
        finish(2, 0, h, total(0, h))
    settle()
    for h in range(2):
        finish(0, 1, 1 - h, total(1, 1 - h) + came(0, 2, 1 - h))
        finish(1, -1, h, total(7, h) + came(1, 2, h))
    for t in range(QUAD):
        for i in (2, 0, 1):
            here = final_vm.at[i, t]
            arrival = remote(here, here, last_send.at[i, t], last_recv.at[i, t], device(dp, z, r ^ 1))
            if i != 2:
                arrival.wait_recv()
            else:
                @pl.when(t != r)
                def _():
                    arrival.wait_recv()
        value = sum(final_vm[i, t].astype(F32) for i in range(3))
        out = vgrad_ref if t % 2 else kgrad_ref
        out[:, (t // 2) * HD : (t // 2 + 1) * HD] = (value * 0.5).astype(BF16)
    for p in range(QUAD):
        @pl.when(p != r)
        def _():
            here = last_vm.at[2, p]
            remote(here, here, last_send.at[2, p], last_recv.at[2, p], device(dp, z, r ^ 1)).wait_send()
    for copy in sends:
        copy.wait_send()
    for d in order:
        gifts[d].wait_send()
    for copy in heads:
        copy.wait()


ANY = pl.BlockSpec(memory_space=pl.ANY)
VMEM = pl.BlockSpec(memory_space=pltpu.VMEM)
DMA = pltpu.SemaphoreType.DMA
LIMIT = 60


def local(query, keys, values, attn_out, grad_out, log_total, doc_lengths, block_order):
    halves = pl.pallas_call(
        kernel,
        out_shape=(
            jax.ShapeDtypeStruct((ROWS, HEADS * HD), BF16),
            jax.ShapeDtypeStruct((ROWS, GROUPS * HD), BF16),
            jax.ShapeDtypeStruct((ROWS, GROUPS * HD), BF16),
        ),
        in_specs=[ANY] * 8,
        out_specs=(ANY, VMEM, VMEM),
        scratch_shapes=[
            pltpu.VMEM((ROWS, HEADS * HD), BF16),
            pltpu.VMEM((ROWS, HEADS * HD), BF16),
            pltpu.VMEM((2, GROUPS, 2, HALF, HD), BF16),
            pltpu.VMEM((HEADS, ROWS), F32),
            pltpu.VMEM((2, 2, QUAD, LANES), F32),
            pltpu.VMEM((SHARD, COLS), BF16),
            pltpu.VMEM((SHARD, COLS), BF16),
            pltpu.VMEM((2, BLOCKS, HALF, HD), BF16),
            pltpu.VMEM((QUAD, 2, 2, QUAD, LANES), F32),
            pltpu.SMEM((NDOC,), jnp.int32),
            pltpu.SMEM((BLOCKS,), jnp.int32),
            pltpu.VMEM((BLOCKS_HERE, HD), jnp.int32),
            pltpu.SMEM((BLOCKS_HERE, HD), jnp.int32),
            pltpu.VMEM((BLOCKS_HERE, 1, LANES), jnp.int32),
            pltpu.VMEM((2, BLOCKS_HERE, WINDOW + 2, HALF, HD), F32),
            pltpu.VMEM((BLOCKS_HERE, WINDOW * HALF, LANES), BF16),
            pltpu.VMEM((SHARD, COLS), BF16),
            pltpu.VMEM((SEQ, HD), F32),
            pltpu.VMEM((SEQ, HD), BF16),
            pltpu.VMEM((SEQ, HD), BF16),
            pltpu.VMEM((2, 3, 2, 2 * ROWS, HD), BF16),
            pltpu.VMEM((2, 3, 2, 2 * ROWS, HD), BF16),
            pltpu.VMEM((3, QUAD, ROWS, HD), BF16),
            pltpu.VMEM((3, QUAD, ROWS, HD), BF16),
            DMA((6,)),
            DMA((8,)),
            DMA((3, QUAD)),
            DMA,
            DMA((3, QUAD)),
            DMA((RING, 2)),
            DMA((RING + 1,)),
            DMA((2, RING, 2)),
            DMA((RING + 1,)),
            DMA((3, QUAD)),
            DMA((3, QUAD)),
            DMA((3,)),
            DMA((RING,)),
            DMA((RING,)),
            DMA((2, 3, 2)),
            DMA((2, 3, 2)),
            DMA((3, QUAD)),
            DMA((3, QUAD)),
            DMA((QUAD,)),
            DMA((QUAD,)),
            DMA,
        ],
        compiler_params=pltpu.CompilerParams(
            collective_id=0, has_side_effects=True, vmem_limit_bytes=LIMIT * 2**20
        ),
    )(query, keys, values, attn_out, grad_out, log_total, doc_lengths, block_order)
    return tuple(half * 2 for half in halves)


def solution(mesh):
    rows = P(("dp", "ctx"), None)
    return jax.shard_map(
        local,
        mesh=mesh,
        in_specs=(rows, rows, rows, rows, rows, P(None, ("dp", "ctx")), P("dp"), P("dp")),
        out_specs=(rows, rows, rows),
        check_vma=False,
    )
```

```python
import functools

import jax
import jax.numpy as jnp
from jax import lax
from jax.experimental import pallas as pl
from jax.experimental.pallas import tpu as pltpu
from jax.sharding import PartitionSpec as P

HD = 128
HEADS = 16
GROUPS = 2
HALF = 64
ROWS = 128
QUAD = 4
RING = 8
SEQ = ROWS * QUAD * RING
SHARD = ROWS * QUAD
COLS = HEADS * HD // QUAD
MEMBER_HEADS = HEADS // QUAD
WINDOW = 1024 // HALF + 1
TILES = ((0, WINDOW),)
NDOC = 16
BLOCKS = SEQ // HALF
BLOCKS_HERE = SHARD // HALF
LANES = MEMBER_HEADS * HALF
MESH = pl.DeviceIdType.MESH
INV_ROOT = HD ** (-0.5)
LOG2E = 1.4426950408889634
F32 = jnp.float32
BF16 = jnp.bfloat16


def place():
    me = lax.axis_index("ctx")
    return lax.axis_index("dp"), me // QUAD, lax.rem(me, QUAD)


def device(dp, z, member):
    return (dp, lax.rem(z + RING, RING) * QUAD + member)


def greet(dp, z, r):
    barrier = pltpu.get_barrier_semaphore()
    for dz in (1, -1):
        for t in range(QUAD):
            pl.semaphore_signal(barrier, inc=1, device_id=device(dp, z + dz, t), device_id_type=MESH)
    for other in range(1, QUAD):
        pl.semaphore_signal(barrier, inc=1, device_id=device(dp, z, r ^ other), device_id_type=MESH)
    return lambda: pl.semaphore_wait(barrier, 2 * QUAD + QUAD - 1)


def rows_at(start, count):
    return pl.ds(pl.multiple_of(start, count), count)


def remote(src, dst, send_sem, recv_sem, target):
    return pltpu.make_async_remote_copy(
        src_ref=src, dst_ref=dst, send_sem=send_sem, recv_sem=recv_sem, device_id=target, device_id_type=MESH
    )


def split_lanes(table, half):
    pieces = []
    for t in range(QUAD):
        heads = [
            table[t * MEMBER_HEADS + e : t * MEMBER_HEADS + e + 1, half * HALF : (half + 1) * HALF]
            for e in range(MEMBER_HEADS)
        ]
        pieces.append(jnp.concatenate(heads, axis=1))
    return jnp.concatenate(pieces, axis=0)


def dot_tt(a, b):
    return lax.dot_general(a, b, (((1,), (1,)), ((), ())), preferred_element_type=F32)


def attend(z, r, qg_ref, dog_ref, kv_ref, ld_ref, order_sm, slot_sm, begin_vm, part_vm, ds_vm, wait_far):
    @pl.loop(0, BLOCKS_HERE)
    def _(i):
        @pl.when(i == BLOCKS_HERE // 2)
        def _():
            wait_far()

        block = lax.rem(i + (r // 2) * (BLOCKS_HERE // 2), BLOCKS_HERE)
        b = order_sm[z * BLOCKS_HERE + block]
        tok_q = b * HALF + lax.broadcasted_iota(jnp.int32, (1, LANES), 1) % HALF
        begin_q = begin_vm[block]
        rows = rows_at(block * HALF, HALF)
        q = jnp.concatenate([qg_ref[rows, e * HD : (e + 1) * HD] for e in range(MEMBER_HEADS)], axis=0)
        do = jnp.concatenate([dog_ref[rows, e * HD : (e + 1) * HD] for e in range(MEMBER_HEADS)], axis=0)
        lse = ld_ref[block // 2, 0, lax.rem(block, 2), pl.ds(r, 1), :]
        delta = ld_ref[block // 2, 1, lax.rem(block, 2), pl.ds(r, 1), :]
        for first, last in TILES:
            base = b - (WINDOW - 1) + first
            places = [slot_sm[block, j] for j in range(first, last)]
            k = jnp.concatenate([kv_ref[0, place] for place in places], axis=0)
            v = jnp.concatenate([kv_ref[1, place] for place in places], axis=0)
            tok_k = base * HALF + lax.broadcasted_iota(jnp.int32, ((last - first) * HALF, 1), 0)
            visible = (tok_k <= tok_q) & (tok_k >= begin_q)
            score = dot_tt(k, q)
            probs = jnp.exp2(jnp.where(visible, score * (INV_ROOT * LOG2E) - lse, -1e30))
            dprobs = dot_tt(v, do)
            dscore = (probs * (dprobs - delta)).astype(BF16)
            probs_low = probs.astype(BF16)
            there = slice(first + 1, last + 1)
            blocks = (last - first, HALF, HD)
            part_vm[1, block, there] = jnp.dot(probs_low, do, preferred_element_type=F32).reshape(blocks)
            part_vm[0, block, there] = jnp.dot(dscore, q, preferred_element_type=F32).reshape(blocks)
            ds_vm[block, first * HALF : last * HALF, :] = dscore


def kernel(
    q_ref, k_ref, v_ref, o_ref, do_ref, lse_ref, doc_ref, order_ref,
    qgrad_ref, kgrad_ref, vgrad_ref,
    o_vm, do_vm, own_kv, lse_vm, ld_vm, qg_ref, dog_ref, kv_ref, ld_ref,
    doc_sm, order_sm, slot_vm, slot_sm, begin_vm, part_vm, ds_vm, dq_ref,
    own_vm, give_vm, other_vm, extra_vm, recv_vm, send_vm, last_vm, final_vm,
    load_sem, own_sem, first_send, first_own, first_recv, half_recv, other_recv, ring_send, core_send, head_send, head_recv, head_own,
    give_send, give_recv, extra_send, extra_recv, sum_send, sum_recv, last_send, last_recv, back_send, back_recv, back_own,
):
    dp, z, r = place()
    core = lax.rem(r, 2)
    greeted = greet(dp, z, r)
    loads = [
        pltpu.make_async_copy(o_ref, o_vm, load_sem.at[0]),
        pltpu.make_async_copy(do_ref, do_vm, load_sem.at[1]),
        pltpu.make_async_copy(lse_ref, lse_vm, load_sem.at[2]),
        pltpu.make_async_copy(doc_ref, doc_sm, load_sem.at[3]),
        pltpu.make_async_copy(order_ref, order_sm, load_sem.at[4]),
    ]
    own = []
    for i, (source, kind, g, half) in enumerate(
        (ref, kind, g, half) for kind, ref in ((0, k_ref), (1, v_ref)) for g in range(GROUPS) for half in range(2)
    ):
        block = source.at[half * HALF : (half + 1) * HALF, g * HD : (g + 1) * HD]
        own.append(pltpu.make_async_copy(block, own_kv.at[kind, g, half], own_sem.at[i]))
    for c in own + loads:
        c.start()
    for c in loads[:3]:
        c.wait()
    prod = do_vm[...].astype(F32) * o_vm[...].astype(F32)
    high = prod.astype(BF16)
    low = (prod - high.astype(F32)).astype(BF16)
    head_of = lax.broadcasted_iota(jnp.int32, (HEADS, HEADS * HD), 1) // HD
    ones = (head_of == lax.broadcasted_iota(jnp.int32, (HEADS, HEADS * HD), 0)).astype(BF16)
    along = (((1,), (1,)), ((), ()))
    delta = lax.dot_general(ones, high, along, preferred_element_type=F32) + lax.dot_general(
        ones, low, along, preferred_element_type=F32
    )
    for half in range(2):
        ld_vm[0, half] = split_lanes(lse_vm[...] * LOG2E, half)
        ld_vm[1, half] = split_lanes(delta, half)
    for c in own:
        c.wait()
    greeted()

    def kv_rows(shard, member):
        return pl.ds((lax.rem(shard + RING, RING) * QUAD + member) * 2, 2)

    first = []
    mine = kv_rows(z, r)
    for i, dz in enumerate((1, -1, 0)):
        for t in range(QUAD):
            source = own_kv.at[t % 2, t // 2]
            target = kv_ref.at[t % 2, mine]
            copy = remote(source, target, first_send.at[i, t], first_recv.at[i, r], device(dp, z + dz, t))
            if i != 2:
                copy.start()
                first.append(copy)
            else:
                @pl.when(t != r)
                def _():
                    copy.start()

                @pl.when(t == r)
                def _():
                    pltpu.make_async_copy(source, target, first_own).start()

    near_heads = []
    far_heads = []
    for i, (src, dst) in enumerate(((q_ref, qg_ref), (do_ref, dog_ref))):
        to_rows = rows_at(r * ROWS, ROWS)
        for other in range(1, QUAD):
            t = r ^ other
            cols = rows_at(t * COLS, COLS)
            copy = remote(
                src.at[:, cols], dst.at[to_rows, :], head_send.at[i, other], head_recv.at[i, other], device(dp, z, t)
            )
            copy.start()
            (near_heads if other == 1 else far_heads).append(copy)
        own = pltpu.make_async_copy(src.at[:, rows_at(r * COLS, COLS)], dst.at[to_rows, :], head_own.at[i])
        own.start()
        near_heads.append(own)

    for other in range(1, QUAD):
        copy = remote(ld_vm, ld_ref.at[r], head_send.at[2, other], head_recv.at[2, other], device(dp, z, r ^ other))
        copy.start()
        (near_heads if other == 1 else far_heads).append(copy)
    own = pltpu.make_async_copy(ld_vm, ld_ref.at[r], head_own.at[2])
    own.start()
    near_heads.append(own)

    forwards = []
    crossings = []

    def half_of(k, h):
        return kv_ref.at[core, pl.ds((lax.rem(z - k + RING, RING) * 2 + h) * QUAD, QUAD)]

    def first_arrived(i, pieces):
        for p in pieces:
            there = kv_ref.at[core, kv_rows(z, p)]
            arrival = remote(there, there, first_send.at[i, 0], first_recv.at[i, p], device(dp, z, r ^ 1))
            if i < 2:
                arrival.wait_recv()
            else:
                @pl.when(p != r)
                def _():
                    arrival.wait_recv()

                @pl.when(p == r)
                def _():
                    pltpu.make_async_copy(there, there, first_own).wait()

    def arrived(k, h):
        there = half_of(k, h)
        remote(there, there, ring_send.at[0, k, h], half_recv.at[k, h], device(dp, z, r ^ 1)).wait_recv()

    def forward(i, k, h):
        step = 1 - 2 * i
        there = half_of(k, h)
        copy = remote(there, there, ring_send.at[i, k, h], half_recv.at[k + step, h], device(dp, z + step, r))
        copy.start()
        forwards.append(copy)

    def crossed(kind, k, h=None):
        zk = lax.rem(z - k + RING, RING)
        if h is None:
            there = kv_ref.at[kind, pl.ds(zk * BLOCKS_HERE, BLOCKS_HERE)]
        else:
            there = kv_ref.at[kind, pl.ds((zk * 2 + h) * QUAD, QUAD)]
        at = k if not h else RING
        return remote(there, there, core_send.at[at], other_recv.at[at], device(dp, z, r ^ 1))

    def cross(k, h=None):
        copy = crossed(core, k, h)
        copy.start()
        crossings.append((copy, k, h))

    for h in range(2):
        for i, hi in ((0, h), (1, 1 - h)):
            first_arrived(i, (2 * hi, 2 * hi + 1))
            forward(i, 1 if i == 0 else RING - 1, hi)
    cross(1)
    cross(RING - 1)
    first_arrived(2, range(QUAD))
    cross(0)
    for c in loads[3:]:
        c.wait()
    wanted = jnp.concatenate(
        [jnp.full((1, HD), order_sm[z * BLOCKS_HERE + block], jnp.int32) for block in range(BLOCKS_HERE)], axis=0
    )
    wanted = wanted - (WINDOW - 1) + lax.broadcasted_iota(jnp.int32, (BLOCKS_HERE, HD), 1)
    slots = lax.fori_loop(
        0, BLOCKS, lambda i, found: jnp.where(wanted == order_sm[i], i, found), jnp.zeros_like(wanted)
    )
    slot_vm[...] = slots
    to_scalars = pltpu.make_async_copy(slot_vm, slot_sm, load_sem.at[5])
    to_scalars.start()
    for h in range(2):
        for i, k, hi in ((0, 2, h), (1, RING - 2, 1 - h)):
            arrived(k, hi)
            forward(i, k, hi)
    cross(2)
    cross(RING - 2)
    within = lax.broadcasted_iota(jnp.int32, (1, LANES), 1) % HALF

    @pl.loop(0, BLOCKS_HERE)
    def _(block):
        tok_q = order_sm[z * BLOCKS_HERE + block] * HALF + within
        begin_q = jnp.zeros((1, LANES), jnp.int32)
        end = jnp.int32(0)
        for d in range(NDOC):
            end = end + doc_sm[d]
            begin_q = jnp.where(end <= tok_q, end, begin_q)
        begin_vm[block] = begin_q
        for kind in range(2):
            part_vm[kind, block, 0] = jnp.zeros((HALF, HD), F32)
            part_vm[kind, block, WINDOW + 1] = jnp.zeros((HALF, HD), F32)
    to_scalars.wait()
    for h in range(2):
        for i, k, hi in ((0, 3, h), (1, RING - 3, 1 - h)):
            arrived(k, hi)
            if h == 0:
                forward(i, k, hi)
    cross(3)
    cross(RING - 3)
    for h in range(2):
        arrived(4, h)
        cross(4, h)
    for _, k, h in crossings:
        crossed(1 - core, k, h).wait_recv()
    for copy in near_heads:
        copy.wait()

    def wait_far_heads():
        for copy in far_heads:
            copy.wait()

    attend(z, r, qg_ref, dog_ref, kv_ref, ld_ref, order_sm, slot_sm, begin_vm, part_vm, ds_vm, wait_far_heads)
    def settle():
        for copy, _, _ in crossings:
            copy.wait_send()
        for copy in forwards + first:
            copy.wait_send()
        for t in range(QUAD):
            @pl.when(t != r)
            def _():
                there = kv_ref.at[0, kv_rows(z, 0)]
                remote(there, there, first_send.at[2, t], first_recv.at[2, 0], device(dp, z, r ^ 1)).wait_send()

    def shard(d):
        return rows_at(lax.rem(z + d + RING, RING) * SHARD, SHARD)

    def piece(d, p):
        return rows_at((lax.rem(z + d + RING, RING) * 2 + p) * ROWS * 2, ROWS * 2)

    order = (4, 3, 5, 2, 6, 1, 7, 0)
    gifts = {}

    def combine(d):
        start = lax.rem(z + d + RING, RING) * BLOCKS_HERE

        @pl.loop(0, BLOCKS_HERE, unroll=2)
        def _(i):
            kb = order_sm[start + i]
            places = []
            for block in range(BLOCKS_HERE):
                at = kb - order_sm[z * BLOCKS_HERE + block] + (WINDOW - 1)
                places.append(jnp.clip(at + 1, 0, WINDOW + 1))
            rows = rows_at((start + i) * HALF, HALF)
            for out, kind in ((give_vm, 1 - core), (own_vm, core)):
                terms = [part_vm[kind, block, places[block]] for block in range(BLOCKS_HERE)]
                while len(terms) > 1:
                    terms = [x + y for x, y in zip(terms[::2], terms[1::2])]
                out[rows, :] = (terms[0] * jnp.where(kind == 0, INV_ROOT, 1.0)).astype(out.dtype)

        if d == 4:
            return
        gifts[d] = remote(
            give_vm.at[shard(d), :], other_vm.at[shard(d), :], give_send.at[d], give_recv.at[d], device(dp, z, r ^ 1)
        )
        gifts[d].start()

    heads = []
    to_cols = rows_at(r * COLS, COLS)

    def query_terms(first_member):
        @pl.loop(0, BLOCKS_HERE // 2)
        def _(i):
            block = first_member * 2 + i
            k = jnp.concatenate([kv_ref[0, slot_sm[block, j]] for j in range(WINDOW)], axis=0)
            dqt = lax.dot_general(k, ds_vm[block], (((0,), (0,)), ((), ())), preferred_element_type=F32)
            dq = (dqt.T * (INV_ROOT * 0.5)).astype(BF16)
            for e in range(MEMBER_HEADS):
                dq_ref[rows_at(block * HALF, HALF), e * HD : (e + 1) * HD] = dq[e * HALF : (e + 1) * HALF]

    def send_back(other):
        t = r ^ other
        copy = remote(
            dq_ref.at[rows_at(t * ROWS, ROWS), :], qgrad_ref.at[:, to_cols],
            back_send.at[other], back_recv.at[other], device(dp, z, t),
        )
        copy.start()
        heads.append(copy)

    def total(d, p):
        return own_vm[piece(d, p), :] + other_vm[piece(d, p), :].astype(F32)

    def ready(d):
        gifts[d].wait_recv()

    sends = []

    def pass_on(i, s, p, value):
        here = send_vm.at[i, s, p]
        here[...] = value.astype(BF16)
        copy = remote(
            here, recv_vm.at[i, s, p], sum_send.at[i, s, p], sum_recv.at[i, s, p],
            device(dp, z + (1 - 2 * i), r),
        )
        copy.start()
        sends.append(copy)

    def came(i, s, p):
        here = recv_vm.at[i, s, p]
        remote(here, here, sum_send.at[i, s, p], sum_recv.at[i, s, p], device(dp, z, r ^ 1)).wait_recv()
        return here[...].astype(F32)

    def far_gift(i, h):
        return remote(
            give_vm.at[piece(4, h), :], extra_vm.at[i], extra_send.at[i], extra_recv.at[i],
            device(dp, z + (1 - 2 * i), r ^ 1),
        )

    combine(4)
    pass_on(0, 0, 0, own_vm[piece(4, 0), :])
    pass_on(1, 0, 1, own_vm[piece(4, 1), :])
    for i in range(2):
        copy = far_gift(i, i)
        copy.start()
        sends.append(copy)
    combine(3)
    combine(5)
    ready(3)
    ready(5)
    pass_on(0, 1, 1, total(3, 1))
    pass_on(1, 1, 0, total(5, 0))
    combine(2)
    combine(6)
    query_terms((1 - r // 2) * 2)
    send_back(2)
    send_back(3)
    for i, d in ((0, 3), (1, 5)):
        value = total(d, i) + came(i, 0, i)
        far_gift(i, i).wait_recv()
        pass_on(i, 1, i, value + extra_vm[i].astype(F32))
    ready(2)
    ready(6)
    for h in range(2):
        pass_on(0, 2, 1 - h, total(2, 1 - h) + came(0, 1, 1 - h))
        pass_on(1, 2, h, total(6, h) + came(1, 1, h))
    combine(1)
    combine(7)
    combine(0)
    query_terms((r // 2) * 2)
    send_back(1)
    own = pltpu.make_async_copy(dq_ref.at[rows_at(r * ROWS, ROWS), :], qgrad_ref.at[:, to_cols], back_own)
    own.start()
    heads.append(own)
    ready(1)
    ready(7)
    ready(0)

    def finish(i, d, h, value):
        for p in (2 * h, 2 * h + 1):
            here = last_vm.at[i, p]
            here[...] = value[(p - 2 * h) * ROWS : (p - 2 * h + 1) * ROWS].astype(BF16)
            there = final_vm.at[i, r]
            copy = remote(here, there, last_send.at[i, p], last_recv.at[i, r], device(dp, z + d, p))
            if d:
                copy.start()
                sends.append(copy)
            else:
                @pl.when(p != r)
                def _():
                    copy.start()

                @pl.when(p == r)
                def _():
                    there[...] = here[...]

    for h in range(2):
        finish(2, 0, h, total(0, h))
    settle()
    for h in range(2):
        finish(0, 1, 1 - h, total(1, 1 - h) + came(0, 2, 1 - h))
        finish(1, -1, h, total(7, h) + came(1, 2, h))
    for t in range(QUAD):
        for i in (2, 0, 1):
            here = final_vm.at[i, t]
            arrival = remote(here, here, last_send.at[i, t], last_recv.at[i, t], device(dp, z, r ^ 1))
            if i != 2:
                arrival.wait_recv()
            else:
                @pl.when(t != r)
                def _():
                    arrival.wait_recv()
        value = sum(final_vm[i, t].astype(F32) for i in range(3))
        out = vgrad_ref if t % 2 else kgrad_ref
        out[:, (t // 2) * HD : (t // 2 + 1) * HD] = (value * 0.5).astype(BF16)
    for p in range(QUAD):
        @pl.when(p != r)
        def _():
            here = last_vm.at[2, p]
            remote(here, here, last_send.at[2, p], last_recv.at[2, p], device(dp, z, r ^ 1)).wait_send()
    for copy in sends:
        copy.wait_send()
    for d in order[1:]:
        gifts[d].wait_send()
    for copy in heads:
        copy.wait()


ANY = pl.BlockSpec(memory_space=pl.ANY)
VMEM = pl.BlockSpec(memory_space=pltpu.VMEM)
DMA = pltpu.SemaphoreType.DMA
LIMIT = 60


def local(query, keys, values, attn_out, grad_out, log_total, doc_lengths, block_order):
    halves = pl.pallas_call(
        kernel,
        out_shape=(
            jax.ShapeDtypeStruct((ROWS, HEADS * HD), BF16),
            jax.ShapeDtypeStruct((ROWS, GROUPS * HD), BF16),
            jax.ShapeDtypeStruct((ROWS, GROUPS * HD), BF16),
        ),
        in_specs=[ANY] * 8,
        out_specs=(ANY, VMEM, VMEM),
        scratch_shapes=[
            pltpu.VMEM((ROWS, HEADS * HD), BF16),
            pltpu.VMEM((ROWS, HEADS * HD), BF16),
            pltpu.VMEM((2, GROUPS, 2, HALF, HD), BF16),
            pltpu.VMEM((HEADS, ROWS), F32),
            pltpu.VMEM((2, 2, QUAD, LANES), F32),
            pltpu.VMEM((SHARD, COLS), BF16),
            pltpu.VMEM((SHARD, COLS), BF16),
            pltpu.VMEM((2, BLOCKS, HALF, HD), BF16),
            pltpu.VMEM((QUAD, 2, 2, QUAD, LANES), F32),
            pltpu.SMEM((NDOC,), jnp.int32),
            pltpu.SMEM((BLOCKS,), jnp.int32),
            pltpu.VMEM((BLOCKS_HERE, HD), jnp.int32),
            pltpu.SMEM((BLOCKS_HERE, HD), jnp.int32),
            pltpu.VMEM((BLOCKS_HERE, 1, LANES), jnp.int32),
            pltpu.VMEM((2, BLOCKS_HERE, WINDOW + 2, HALF, HD), F32),
            pltpu.VMEM((BLOCKS_HERE, WINDOW * HALF, LANES), BF16),
            pltpu.VMEM((SHARD, COLS), BF16),
            pltpu.VMEM((SEQ, HD), F32),
            pltpu.VMEM((SEQ, HD), BF16),
            pltpu.VMEM((SEQ, HD), BF16),
            pltpu.VMEM((2, 2 * ROWS, HD), BF16),
            pltpu.VMEM((2, 3, 2, 2 * ROWS, HD), BF16),
            pltpu.VMEM((2, 3, 2, 2 * ROWS, HD), BF16),
            pltpu.VMEM((3, QUAD, ROWS, HD), BF16),
            pltpu.VMEM((3, QUAD, ROWS, HD), BF16),
            DMA((6,)),
            DMA((8,)),
            DMA((3, QUAD)),
            DMA,
            DMA((3, QUAD)),
            DMA((RING, 2)),
            DMA((RING + 1,)),
            DMA((2, RING, 2)),
            DMA((RING + 1,)),
            DMA((3, QUAD)),
            DMA((3, QUAD)),
            DMA((3,)),
            DMA((RING,)),
            DMA((RING,)),
            DMA((2,)),
            DMA((2,)),
            DMA((2, 3, 2)),
            DMA((2, 3, 2)),
            DMA((3, QUAD)),
            DMA((3, QUAD)),
            DMA((QUAD,)),
            DMA((QUAD,)),
            DMA,
        ],
        compiler_params=pltpu.CompilerParams(
            collective_id=0, has_side_effects=True, vmem_limit_bytes=LIMIT * 2**20
        ),
    )(query, keys, values, attn_out, grad_out, log_total, doc_lengths, block_order)
    return tuple(half * 2 for half in halves)


def solution(mesh):
    rows = P(("dp", "ctx"), None)
    return jax.shard_map(
        local,
        mesh=mesh,
        in_specs=(rows, rows, rows, rows, rows, P(None, ("dp", "ctx")), P("dp"), P("dp")),
        out_specs=(rows, rows, rows),
        check_vma=False,
    )
```

```python
import functools

import jax
import jax.numpy as jnp
from jax import lax
from jax.experimental import pallas as pl
from jax.experimental.pallas import tpu as pltpu
from jax.sharding import PartitionSpec as P

HD = 128
HEADS = 16
GROUPS = 2
HALF = 64
ROWS = 128
QUAD = 4
RING = 8
SEQ = ROWS * QUAD * RING
SHARD = ROWS * QUAD
COLS = HEADS * HD // QUAD
MEMBER_HEADS = HEADS // QUAD
WINDOW = 1024 // HALF + 1
TILES = ((0, WINDOW),)
NDOC = 16
BLOCKS = SEQ // HALF
BLOCKS_HERE = SHARD // HALF
LANES = MEMBER_HEADS * HALF
MESH = pl.DeviceIdType.MESH
INV_ROOT = HD ** (-0.5)
LOG2E = 1.4426950408889634
F32 = jnp.float32
BF16 = jnp.bfloat16


def place():
    me = lax.axis_index("ctx")
    return lax.axis_index("dp"), me // QUAD, lax.rem(me, QUAD)


def device(dp, z, member):
    return (dp, lax.rem(z + RING, RING) * QUAD + member)


def greet(dp, z, r):
    barrier = pltpu.get_barrier_semaphore()
    for dz in (1, -1):
        for t in range(QUAD):
            pl.semaphore_signal(barrier, inc=1, device_id=device(dp, z + dz, t), device_id_type=MESH)
    for other in range(1, QUAD):
        pl.semaphore_signal(barrier, inc=1, device_id=device(dp, z, r ^ other), device_id_type=MESH)
    return lambda: pl.semaphore_wait(barrier, 2 * QUAD + QUAD - 1)


def rows_at(start, count):
    return pl.ds(pl.multiple_of(start, count), count)


def remote(src, dst, send_sem, recv_sem, target):
    return pltpu.make_async_remote_copy(
        src_ref=src, dst_ref=dst, send_sem=send_sem, recv_sem=recv_sem, device_id=target, device_id_type=MESH
    )


def split_lanes(table, half):
    pieces = []
    for t in range(QUAD):
        heads = [
            table[t * MEMBER_HEADS + e : t * MEMBER_HEADS + e + 1, half * HALF : (half + 1) * HALF]
            for e in range(MEMBER_HEADS)
        ]
        pieces.append(jnp.concatenate(heads, axis=1))
    return jnp.concatenate(pieces, axis=0)


def dot_tt(a, b):
    return lax.dot_general(a, b, (((1,), (1,)), ((), ())), preferred_element_type=F32)


def attend(z, r, qg_ref, dog_ref, kv_ref, ld_ref, order_sm, slot_sm, begin_vm, part_vm, ds_vm, wait_far):
    @pl.loop(0, BLOCKS_HERE)
    def _(i):
        @pl.when(i == BLOCKS_HERE // 2)
        def _():
            wait_far()

        block = lax.rem(i + (r // 2) * (BLOCKS_HERE // 2), BLOCKS_HERE)
        b = order_sm[z * BLOCKS_HERE + block]
        tok_q = b * HALF + lax.broadcasted_iota(jnp.int32, (1, LANES), 1) % HALF
        begin_q = begin_vm[block]
        rows = rows_at(block * HALF, HALF)
        q = jnp.concatenate([qg_ref[rows, e * HD : (e + 1) * HD] for e in range(MEMBER_HEADS)], axis=0)
        do = jnp.concatenate([dog_ref[rows, e * HD : (e + 1) * HD] for e in range(MEMBER_HEADS)], axis=0)
        lse = ld_ref[block // 2, 0, lax.rem(block, 2), pl.ds(r, 1), :]
        delta = ld_ref[block // 2, 1, lax.rem(block, 2), pl.ds(r, 1), :]
        for first, last in TILES:
            base = b - (WINDOW - 1) + first
            places = [slot_sm[block, j] for j in range(first, last)]
            k = jnp.concatenate([kv_ref[0, place] for place in places], axis=0)
            v = jnp.concatenate([kv_ref[1, place] for place in places], axis=0)
            tok_k = base * HALF + lax.broadcasted_iota(jnp.int32, ((last - first) * HALF, 1), 0)
            visible = (tok_k <= tok_q) & (tok_k >= begin_q)
            score = dot_tt(k, q)
            probs = jnp.exp2(jnp.where(visible, score * (INV_ROOT * LOG2E) - lse, -1e30))
            dprobs = dot_tt(v, do)
            dscore = (probs * (dprobs - delta)).astype(BF16)
            probs_low = probs.astype(BF16)
            there = slice(first + 1, last + 1)
            blocks = (last - first, HALF, HD)
            part_vm[1, block, there] = jnp.dot(probs_low, do, preferred_element_type=F32).reshape(blocks)
            part_vm[0, block, there] = jnp.dot(dscore, q, preferred_element_type=F32).reshape(blocks)
            ds_vm[block, first * HALF : last * HALF, :] = dscore


def kernel(
    q_ref, k_ref, v_ref, o_ref, do_ref, lse_ref, doc_ref, order_ref,
    qgrad_ref, kgrad_ref, vgrad_ref,
    o_vm, do_vm, own_kv, lse_vm, ld_vm, qg_ref, dog_ref, kv_ref, ld_ref,
    doc_sm, order_sm, slot_vm, slot_sm, begin_vm, part_vm, ds_vm, dq_ref,
    own_vm, give_vm, other_vm, extra_vm, recv_vm, send_vm, last_vm, final_vm,
    load_sem, own_sem, first_send, first_own, first_recv, half_recv, other_recv, ring_send, core_send, head_send, head_recv, head_own,
    give_send, give_recv, extra_send, extra_recv, sum_send, sum_recv, last_send, last_recv, back_send, back_recv, back_own,
):
    dp, z, r = place()
    core = lax.rem(r, 2)
    greeted = greet(dp, z, r)
    loads = [
        pltpu.make_async_copy(o_ref, o_vm, load_sem.at[0]),
        pltpu.make_async_copy(do_ref, do_vm, load_sem.at[1]),
        pltpu.make_async_copy(lse_ref, lse_vm, load_sem.at[2]),
        pltpu.make_async_copy(doc_ref, doc_sm, load_sem.at[3]),
        pltpu.make_async_copy(order_ref, order_sm, load_sem.at[4]),
    ]
    own = []
    for i, (source, kind, g, half) in enumerate(
        (ref, kind, g, half) for kind, ref in ((0, k_ref), (1, v_ref)) for g in range(GROUPS) for half in range(2)
    ):
        block = source.at[half * HALF : (half + 1) * HALF, g * HD : (g + 1) * HD]
        own.append(pltpu.make_async_copy(block, own_kv.at[kind, g, half], own_sem.at[i]))
    for c in own + loads:
        c.start()
    for c in loads[:3]:
        c.wait()
    prod = do_vm[...].astype(F32) * o_vm[...].astype(F32)
    high = prod.astype(BF16)
    low = (prod - high.astype(F32)).astype(BF16)
    head_of = lax.broadcasted_iota(jnp.int32, (HEADS, HEADS * HD), 1) // HD
    ones = (head_of == lax.broadcasted_iota(jnp.int32, (HEADS, HEADS * HD), 0)).astype(BF16)
    along = (((1,), (1,)), ((), ()))
    delta = lax.dot_general(ones, high, along, preferred_element_type=F32) + lax.dot_general(
        ones, low, along, preferred_element_type=F32
    )
    for half in range(2):
        ld_vm[0, half] = split_lanes(lse_vm[...] * LOG2E, half)
        ld_vm[1, half] = split_lanes(delta, half)
    for c in own:
        c.wait()
    greeted()

    def kv_rows(shard, member):
        return pl.ds((lax.rem(shard + RING, RING) * QUAD + member) * 2, 2)

    first = []
    mine = kv_rows(z, r)
    for i, dz in enumerate((1, -1, 0)):
        for t in range(QUAD):
            source = own_kv.at[t % 2, t // 2]
            target = kv_ref.at[t % 2, mine]
            copy = remote(source, target, first_send.at[i, t], first_recv.at[i, r], device(dp, z + dz, t))
            if i != 2:
                copy.start()
                first.append(copy)
            else:
                @pl.when(t != r)
                def _():
                    copy.start()

                @pl.when(t == r)
                def _():
                    pltpu.make_async_copy(source, target, first_own).start()

    near_heads = []
    far_heads = []
    for i, (src, dst) in enumerate(((q_ref, qg_ref), (do_ref, dog_ref))):
        to_rows = rows_at(r * ROWS, ROWS)
        for other in range(1, QUAD):
            t = r ^ other
            cols = rows_at(t * COLS, COLS)
            copy = remote(
                src.at[:, cols], dst.at[to_rows, :], head_send.at[i, other], head_recv.at[i, other], device(dp, z, t)
            )
            copy.start()
            (near_heads if other == 1 else far_heads).append(copy)
        own = pltpu.make_async_copy(src.at[:, rows_at(r * COLS, COLS)], dst.at[to_rows, :], head_own.at[i])
        own.start()
        near_heads.append(own)

    for other in range(1, QUAD):
        copy = remote(ld_vm, ld_ref.at[r], head_send.at[2, other], head_recv.at[2, other], device(dp, z, r ^ other))
        copy.start()
        (near_heads if other == 1 else far_heads).append(copy)
    own = pltpu.make_async_copy(ld_vm, ld_ref.at[r], head_own.at[2])
    own.start()
    near_heads.append(own)

    forwards = []
    crossings = []

    def half_of(k, h):
        return kv_ref.at[core, pl.ds((lax.rem(z - k + RING, RING) * 2 + h) * QUAD, QUAD)]

    def first_arrived(i, pieces):
        for p in pieces:
            there = kv_ref.at[core, kv_rows(z, p)]
            arrival = remote(there, there, first_send.at[i, 0], first_recv.at[i, p], device(dp, z, r ^ 1))
            if i < 2:
                arrival.wait_recv()
            else:
                @pl.when(p != r)
                def _():
                    arrival.wait_recv()

                @pl.when(p == r)
                def _():
                    pltpu.make_async_copy(there, there, first_own).wait()

    def arrived(k, h):
        there = half_of(k, h)
        remote(there, there, ring_send.at[0, k, h], half_recv.at[k, h], device(dp, z, r ^ 1)).wait_recv()

    def forward(i, k, h):
        step = 1 - 2 * i
        there = half_of(k, h)
        copy = remote(there, there, ring_send.at[i, k, h], half_recv.at[k + step, h], device(dp, z + step, r))
        copy.start()
        forwards.append(copy)

    def crossed(kind, k, h=None):
        zk = lax.rem(z - k + RING, RING)
        if h is None:
            there = kv_ref.at[kind, pl.ds(zk * BLOCKS_HERE, BLOCKS_HERE)]
        else:
            there = kv_ref.at[kind, pl.ds((zk * 2 + h) * QUAD, QUAD)]
        at = k if not h else RING
        return remote(there, there, core_send.at[at], other_recv.at[at], device(dp, z, r ^ 1))

    def cross(k, h=None):
        copy = crossed(core, k, h)
        copy.start()
        crossings.append((copy, k, h))

    for h in range(2):
        for i, hi in ((0, h), (1, 1 - h)):
            first_arrived(i, (2 * hi, 2 * hi + 1))
            forward(i, 1 if i == 0 else RING - 1, hi)
    cross(1)
    cross(RING - 1)
    first_arrived(2, range(QUAD))
    cross(0)
    for c in loads[3:]:
        c.wait()
    wanted = jnp.concatenate(
        [jnp.full((1, HD), order_sm[z * BLOCKS_HERE + block], jnp.int32) for block in range(BLOCKS_HERE)], axis=0
    )
    wanted = wanted - (WINDOW - 1) + lax.broadcasted_iota(jnp.int32, (BLOCKS_HERE, HD), 1)
    slots = lax.fori_loop(
        0, BLOCKS, lambda i, found: jnp.where(wanted == order_sm[i], i, found), jnp.zeros_like(wanted)
    )
    slot_vm[...] = slots
    to_scalars = pltpu.make_async_copy(slot_vm, slot_sm, load_sem.at[5])
    to_scalars.start()
    for h in range(2):
        for i, k, hi in ((0, 2, h), (1, RING - 2, 1 - h)):
            arrived(k, hi)
            forward(i, k, hi)
    cross(2)
    cross(RING - 2)
    within = lax.broadcasted_iota(jnp.int32, (1, LANES), 1) % HALF

    @pl.loop(0, BLOCKS_HERE)
    def _(block):
        tok_q = order_sm[z * BLOCKS_HERE + block] * HALF + within
        begin_q = jnp.zeros((1, LANES), jnp.int32)
        end = jnp.int32(0)
        for d in range(NDOC):
            end = end + doc_sm[d]
            begin_q = jnp.where(end <= tok_q, end, begin_q)
        begin_vm[block] = begin_q
        for kind in range(2):
            part_vm[kind, block, 0] = jnp.zeros((HALF, HD), F32)
            part_vm[kind, block, WINDOW + 1] = jnp.zeros((HALF, HD), F32)
    to_scalars.wait()
    for h in range(2):
        for i, k, hi in ((0, 3, h), (1, RING - 3, 1 - h)):
            arrived(k, hi)
            if h == 0:
                forward(i, k, hi)
    cross(3)
    cross(RING - 3)
    for h in range(2):
        arrived(4, h)
        cross(4, h)
    for _, k, h in crossings:
        crossed(1 - core, k, h).wait_recv()
    for copy in near_heads:
        copy.wait()

    def wait_far_heads():
        for copy in far_heads:
            copy.wait()

    attend(z, r, qg_ref, dog_ref, kv_ref, ld_ref, order_sm, slot_sm, begin_vm, part_vm, ds_vm, wait_far_heads)
    def settle():
        for copy, _, _ in crossings:
            copy.wait_send()
        for copy in forwards + first:
            copy.wait_send()
        for t in range(QUAD):
            @pl.when(t != r)
            def _():
                there = kv_ref.at[0, kv_rows(z, 0)]
                remote(there, there, first_send.at[2, t], first_recv.at[2, 0], device(dp, z, r ^ 1)).wait_send()

    def shard(d):
        return rows_at(lax.rem(z + d + RING, RING) * SHARD, SHARD)

    def piece(d, p):
        return rows_at((lax.rem(z + d + RING, RING) * 2 + p) * ROWS * 2, ROWS * 2)

    order = (4, 3, 5, 2, 6, 1, 7, 0)
    gifts = {}

    def combine(d):
        start = lax.rem(z + d + RING, RING) * BLOCKS_HERE

        @pl.loop(0, BLOCKS_HERE, unroll=4)
        def _(i):
            kb = order_sm[start + i]
            places = []
            for block in range(BLOCKS_HERE):
                at = kb - order_sm[z * BLOCKS_HERE + block] + (WINDOW - 1)
                places.append(jnp.clip(at + 1, 0, WINDOW + 1))
            rows = rows_at((start + i) * HALF, HALF)
            for out, kind in ((give_vm, 1 - core), (own_vm, core)):
                terms = [part_vm[kind, block, places[block]] for block in range(BLOCKS_HERE)]
                while len(terms) > 1:
                    terms = [x + y for x, y in zip(terms[::2], terms[1::2])]
                out[rows, :] = (terms[0] * jnp.where(kind == 0, INV_ROOT, 1.0)).astype(out.dtype)

        if d == 4:
            return
        gifts[d] = remote(
            give_vm.at[shard(d), :], other_vm.at[shard(d), :], give_send.at[d], give_recv.at[d], device(dp, z, r ^ 1)
        )
        gifts[d].start()

    heads = []
    to_cols = rows_at(r * COLS, COLS)

    def query_terms(first_member):
        @pl.loop(0, BLOCKS_HERE // 2)
        def _(i):
            block = first_member * 2 + i
            k = jnp.concatenate([kv_ref[0, slot_sm[block, j]] for j in range(WINDOW)], axis=0)
            dqt = lax.dot_general(k, ds_vm[block], (((0,), (0,)), ((), ())), preferred_element_type=F32)
            dq = (dqt.T * (INV_ROOT * 0.5)).astype(BF16)
            for e in range(MEMBER_HEADS):
                dq_ref[rows_at(block * HALF, HALF), e * HD : (e + 1) * HD] = dq[e * HALF : (e + 1) * HALF]

    def send_back(other):
        t = r ^ other
        copy = remote(
            dq_ref.at[rows_at(t * ROWS, ROWS), :], qgrad_ref.at[:, to_cols],
            back_send.at[other], back_recv.at[other], device(dp, z, t),
        )
        copy.start()
        heads.append(copy)

    def total(d, p):
        return own_vm[piece(d, p), :] + other_vm[piece(d, p), :].astype(F32)

    def ready(d):
        gifts[d].wait_recv()

    sends = []

    def pass_on(i, s, p, value):
        here = send_vm.at[i, s, p]
        here[...] = value.astype(BF16)
        copy = remote(
            here, recv_vm.at[i, s, p], sum_send.at[i, s, p], sum_recv.at[i, s, p],
            device(dp, z + (1 - 2 * i), r),
        )
        copy.start()
        sends.append(copy)

    def came(i, s, p):
        here = recv_vm.at[i, s, p]
        remote(here, here, sum_send.at[i, s, p], sum_recv.at[i, s, p], device(dp, z, r ^ 1)).wait_recv()
        return here[...].astype(F32)

    def far_gift(i, h):
        return remote(
            give_vm.at[piece(4, h), :], extra_vm.at[i], extra_send.at[i], extra_recv.at[i],
            device(dp, z + (1 - 2 * i), r ^ 1),
        )

    combine(4)
    pass_on(0, 0, 0, own_vm[piece(4, 0), :])
    pass_on(1, 0, 1, own_vm[piece(4, 1), :])
    for i in range(2):
        copy = far_gift(i, i)
        copy.start()
        sends.append(copy)
    combine(3)
    combine(5)
    ready(3)
    ready(5)
    pass_on(0, 1, 1, total(3, 1))
    pass_on(1, 1, 0, total(5, 0))
    combine(2)
    combine(6)
    query_terms((1 - r // 2) * 2)
    send_back(2)
    send_back(3)
    for i, d in ((0, 3), (1, 5)):
        value = total(d, i) + came(i, 0, i)
        far_gift(i, i).wait_recv()
        pass_on(i, 1, i, value + extra_vm[i].astype(F32))
    ready(2)
    ready(6)
    for h in range(2):
        pass_on(0, 2, 1 - h, total(2, 1 - h) + came(0, 1, 1 - h))
        pass_on(1, 2, h, total(6, h) + came(1, 1, h))
    combine(1)
    combine(7)
    combine(0)
    query_terms((r // 2) * 2)
    send_back(1)
    own = pltpu.make_async_copy(dq_ref.at[rows_at(r * ROWS, ROWS), :], qgrad_ref.at[:, to_cols], back_own)
    own.start()
    heads.append(own)
    ready(1)
    ready(7)
    ready(0)

    def finish(i, d, h, value):
        for p in (2 * h, 2 * h + 1):
            here = last_vm.at[i, p]
            here[...] = value[(p - 2 * h) * ROWS : (p - 2 * h + 1) * ROWS].astype(BF16)
            there = final_vm.at[i, r]
            copy = remote(here, there, last_send.at[i, p], last_recv.at[i, r], device(dp, z + d, p))
            if d:
                copy.start()
                sends.append(copy)
            else:
                @pl.when(p != r)
                def _():
                    copy.start()

                @pl.when(p == r)
                def _():
                    there[...] = here[...]

    for h in range(2):
        finish(2, 0, h, total(0, h))
    settle()
    for h in range(2):
        finish(0, 1, 1 - h, total(1, 1 - h) + came(0, 2, 1 - h))
        finish(1, -1, h, total(7, h) + came(1, 2, h))
    for t in range(QUAD):
        for i in (2, 0, 1):
            here = final_vm.at[i, t]
            arrival = remote(here, here, last_send.at[i, t], last_recv.at[i, t], device(dp, z, r ^ 1))
            if i != 2:
                arrival.wait_recv()
            else:
                @pl.when(t != r)
                def _():
                    arrival.wait_recv()
        value = sum(final_vm[i, t].astype(F32) for i in range(3))
        out = vgrad_ref if t % 2 else kgrad_ref
        out[:, (t // 2) * HD : (t // 2 + 1) * HD] = (value * 0.5).astype(BF16)
    for p in range(QUAD):
        @pl.when(p != r)
        def _():
            here = last_vm.at[2, p]
            remote(here, here, last_send.at[2, p], last_recv.at[2, p], device(dp, z, r ^ 1)).wait_send()
    for copy in sends:
        copy.wait_send()
    for d in order[1:]:
        gifts[d].wait_send()
    for copy in heads:
        copy.wait()


ANY = pl.BlockSpec(memory_space=pl.ANY)
VMEM = pl.BlockSpec(memory_space=pltpu.VMEM)
DMA = pltpu.SemaphoreType.DMA
LIMIT = 60


def local(query, keys, values, attn_out, grad_out, log_total, doc_lengths, block_order):
    halves = pl.pallas_call(
        kernel,
        out_shape=(
            jax.ShapeDtypeStruct((ROWS, HEADS * HD), BF16),
            jax.ShapeDtypeStruct((ROWS, GROUPS * HD), BF16),
            jax.ShapeDtypeStruct((ROWS, GROUPS * HD), BF16),
        ),
        in_specs=[ANY] * 8,
        out_specs=(ANY, VMEM, VMEM),
        scratch_shapes=[
            pltpu.VMEM((ROWS, HEADS * HD), BF16),
            pltpu.VMEM((ROWS, HEADS * HD), BF16),
            pltpu.VMEM((2, GROUPS, 2, HALF, HD), BF16),
            pltpu.VMEM((HEADS, ROWS), F32),
            pltpu.VMEM((2, 2, QUAD, LANES), F32),
            pltpu.VMEM((SHARD, COLS), BF16),
            pltpu.VMEM((SHARD, COLS), BF16),
            pltpu.VMEM((2, BLOCKS, HALF, HD), BF16),
            pltpu.VMEM((QUAD, 2, 2, QUAD, LANES), F32),
            pltpu.SMEM((NDOC,), jnp.int32),
            pltpu.SMEM((BLOCKS,), jnp.int32),
            pltpu.VMEM((BLOCKS_HERE, HD), jnp.int32),
            pltpu.SMEM((BLOCKS_HERE, HD), jnp.int32),
            pltpu.VMEM((BLOCKS_HERE, 1, LANES), jnp.int32),
            pltpu.VMEM((2, BLOCKS_HERE, WINDOW + 2, HALF, HD), F32),
            pltpu.VMEM((BLOCKS_HERE, WINDOW * HALF, LANES), BF16),
            pltpu.VMEM((SHARD, COLS), BF16),
            pltpu.VMEM((SEQ, HD), F32),
            pltpu.VMEM((SEQ, HD), BF16),
            pltpu.VMEM((SEQ, HD), BF16),
            pltpu.VMEM((2, 2 * ROWS, HD), BF16),
            pltpu.VMEM((2, 3, 2, 2 * ROWS, HD), BF16),
            pltpu.VMEM((2, 3, 2, 2 * ROWS, HD), BF16),
            pltpu.VMEM((3, QUAD, ROWS, HD), BF16),
            pltpu.VMEM((3, QUAD, ROWS, HD), BF16),
            DMA((6,)),
            DMA((8,)),
            DMA((3, QUAD)),
            DMA,
            DMA((3, QUAD)),
            DMA((RING, 2)),
            DMA((RING + 1,)),
            DMA((2, RING, 2)),
            DMA((RING + 1,)),
            DMA((3, QUAD)),
            DMA((3, QUAD)),
            DMA((3,)),
            DMA((RING,)),
            DMA((RING,)),
            DMA((2,)),
            DMA((2,)),
            DMA((2, 3, 2)),
            DMA((2, 3, 2)),
            DMA((3, QUAD)),
            DMA((3, QUAD)),
            DMA((QUAD,)),
            DMA((QUAD,)),
            DMA,
        ],
        compiler_params=pltpu.CompilerParams(
            collective_id=0, has_side_effects=True, vmem_limit_bytes=LIMIT * 2**20
        ),
    )(query, keys, values, attn_out, grad_out, log_total, doc_lengths, block_order)
    return tuple(half * 2 for half in halves)


def solution(mesh):
    rows = P(("dp", "ctx"), None)
    return jax.shard_map(
        local,
        mesh=mesh,
        in_specs=(rows, rows, rows, rows, rows, P(None, ("dp", "ctx")), P("dp"), P("dp")),
        out_specs=(rows, rows, rows),
        check_vma=False,
    )
```
